256 devices in a mesh: grp: 4 (over y), ext: 64 (over z, x, core).
Axes of the slice: x: 4, y: 4, z: 8, core: 2. Of those that a mesh axis runs over, the one named last changes fastest.
Arguments:
- tiles: bfloat16 [4608, 49, 2048], P(('grp', 'ext')), may hold values from -6 to 6
- tissue_index: int32 [256, 18], P(('grp', 'ext')), may hold values from 0 to 17, each once within a row
- tissue_count: int32 [256], P(('grp', 'ext')), may hold values from 0 to 16, as said below
- w_reduce: bfloat16 [2048, 512], replicated, may hold values from -0.125 to 0.125
- scale_reduce: float32 [512], replicated, may hold values from 0.5 to 2
- bias_reduce: float32 [512], replicated, may hold values from -3 to 3
- w_spatial: bfloat16 [3, 3, 512, 512], replicated, may hold values from -0.09375 to 0.09375
- scale_spatial: float32 [512], replicated, may hold values from 0.5 to 2
- bias_spatial: float32 [512], replicated, may hold values from -3 to 3
- w_expand: bfloat16 [512, 2048], replicated, may hold values from -0.25 to 0.25
- scale_expand: float32 [2048], replicated, may hold values from 0.5 to 2
- bias_expand: float32 [2048], replicated, may hold values from -3 to 3
Outputs:
- embeddings: bfloat16 [2048, 2048], P(('grp', 'ext'))
The draws below stay inside these ranges and needn't reach their ends.
Inputs may be any that keep to these rules, and one draw needn't show every extreme that they name: Let S(d) be the sum of tissue_count over owners before owner d; then 8 * d <= S(d) <= 8 * (d + 1) for every d, and all counts sum to 2048.
All inputs are finite; a program needn't handle non-finite values.
Results may differ from the reference program's by a relative error of at most 0.0021.
Values may be sent and summed in bfloat16 or wider, within the bound.
A program may use at most 128 MiB of HBM per device.

```python
import math
import jax
import jax.numpy as jnp
from jax import lax

C = 2048
MID = 512
SIDE = 7
SEQ_DEV = 8
CAND = 18
OWNERS = 256
TOTAL = 2048


def draw_tissue_count(key, part):
    drift_key = jax.random.fold_in(key, 11)
    drift_vals = jax.random.randint(drift_key, (OWNERS + 1,), 1, SEQ_DEV + 1, dtype=jnp.int32)
    drift_vals = drift_vals.at[1].set(SEQ_DEV).at[OWNERS - 1].set(SEQ_DEV)
    drift_vals = drift_vals.at[0].set(0).at[OWNERS].set(0)
    return (SEQ_DEV + drift_vals[1:] - drift_vals[:-1]).astype(jnp.int32)


def block_levels(own_key, extent, shards, least, largest):
    def one(dim, parts):
        draws = jax.random.uniform(jax.random.fold_in(jax.random.fold_in(own_key, 6), dim), (parts,), jnp.float32, least / len(shards), largest / len(shards))
        return jnp.repeat(jnp.exp(draws), extent[dim] // parts).reshape((-1,) + (1,) * (len(extent) - dim - 1))

    gain = one(*shards[0])
    for cut in shards[1:]:
        gain = gain * one(*cut)
    return gain


def gaussian(own_key, extent, spread, reach, shards=(), kind=jnp.bfloat16):
    array = jax.random.normal(own_key, extent, jnp.float32) * spread
    if len(shards) > 0:
        array = block_levels(own_key, extent, shards, -0.22, 0.18) * array
    return jnp.clip(array, min=-reach, max=reach).astype(kind)


def setup_inputs(seed: int = 0) -> dict:
    seeds = jax.random.split(jax.random.key(seed), 13)
    tiles = gaussian(seeds[0], (OWNERS * CAND, SIDE * SIDE, C), 1.0, 6.0, ((0, 256),))
    tissue_index = jax.vmap(lambda own: jax.random.permutation(own, CAND))(jax.random.split(seeds[1], OWNERS)).reshape((OWNERS, CAND)).astype(jnp.int32)
    tissue_count = draw_tissue_count(jax.random.fold_in(seeds[12], 71), 0)
    w_reduce = gaussian(seeds[3], (C, MID), C ** -0.5, 0.125)
    scale_reduce = jnp.clip(jnp.exp(jax.random.uniform(seeds[4], (MID,), jnp.float32, math.log(0.5), math.log(2.0))), 0.5, 2.0)
    bias_reduce = gaussian(seeds[5], (MID,), 0.5, 3.0, (), jnp.float32)
    w_spatial = gaussian(seeds[6], (3, 3, MID, MID), (9 * MID) ** -0.5, 0.09375)
    scale_spatial = jnp.clip(jnp.exp(jax.random.uniform(seeds[7], (MID,), jnp.float32, math.log(0.5), math.log(2.0))), 0.5, 2.0)
    bias_spatial = gaussian(seeds[8], (MID,), 0.5, 3.0, (), jnp.float32)
    w_expand = gaussian(seeds[9], (MID, C), MID ** -0.5, 0.25)
    scale_expand = jnp.clip(jnp.exp(jax.random.uniform(seeds[10], (C,), jnp.float32, math.log(0.5), math.log(2.0))), 0.5, 2.0)
    bias_expand = gaussian(seeds[11], (C,), 0.5, 3.0, (), jnp.float32)
    return dict(tiles=tiles, tissue_index=tissue_index, tissue_count=tissue_count, w_reduce=w_reduce, scale_reduce=scale_reduce, bias_reduce=bias_reduce, w_spatial=w_spatial, scale_spatial=scale_spatial, bias_spatial=bias_spatial, w_expand=w_expand, scale_expand=scale_expand, bias_expand=bias_expand)


def bottleneck(tile_maps, w_reduce, scale_reduce, bias_reduce, w_spatial, scale_spatial, bias_spatial, w_expand, scale_expand, bias_expand):
    count_tiles = tile_maps.shape[0]
    flat_map = tile_maps.reshape(count_tiles * SIDE * SIDE, C)
    reduced = jnp.maximum(jnp.dot(flat_map, w_reduce, preferred_element_type=jnp.float32) * scale_reduce + bias_reduce, 0.0).astype(jnp.bfloat16)
    grid_map = reduced.reshape(count_tiles, SIDE, SIDE, MID)
    padded = jnp.pad(grid_map, ((0, 0), (1, 1), (1, 1), (0, 0)))
    summed = jnp.zeros((count_tiles * SIDE * SIDE, MID), jnp.float32)
    for row_shift in range(3):
        for col_shift in range(3):
            window = padded[:, row_shift:row_shift + SIDE, col_shift:col_shift + SIDE, :].reshape(count_tiles * SIDE * SIDE, MID)
            summed = summed + jnp.dot(window, w_spatial[row_shift, col_shift], preferred_element_type=jnp.float32)
    spatial = jnp.maximum(summed * scale_spatial + bias_spatial, 0.0).astype(jnp.bfloat16)
    expanded = jnp.maximum(jnp.dot(spatial, w_expand, preferred_element_type=jnp.float32) * scale_expand + bias_expand + flat_map.astype(jnp.float32), 0.0)
    return jnp.mean(expanded.reshape(count_tiles, SIDE * SIDE, C), axis=1).astype(jnp.bfloat16)


def reference(tiles, tissue_index, tissue_count, w_reduce, scale_reduce, bias_reduce, w_spatial, scale_spatial, bias_spatial, w_expand, scale_expand, bias_expand):
    owners = tissue_count.shape[0]
    start = (jnp.cumsum(tissue_count) - tissue_count).astype(jnp.int32)
    slot_ids = jnp.arange(2 * SEQ_DEV, dtype=jnp.int32)
    position = start[:, None] + slot_ids[None, :]
    is_valid = slot_ids[None, :] < tissue_count[:, None]
    source = (jnp.arange(owners, dtype=jnp.int32)[:, None] * CAND + tissue_index[:, :2 * SEQ_DEV]).astype(jnp.int32)
    target = jnp.where(is_valid, position, TOTAL).reshape(-1).astype(jnp.int32)
    source_of = jnp.zeros((TOTAL,), jnp.int32).at[target].set(source.reshape(-1), mode="drop")
    blocks = source_of.reshape(TOTAL // SEQ_DEV, SEQ_DEV)

    def encode_block(tile_ids):
        return bottleneck(tiles[tile_ids], w_reduce, scale_reduce, bias_reduce, w_spatial, scale_spatial, bias_spatial, w_expand, scale_expand, bias_expand)

    encoded = lax.map(encode_block, blocks)
    return encoded.reshape(TOTAL, C)
```

```python
import functools

import jax
import jax.numpy as jnp
from jax import lax
from jax.experimental import pallas as pl
from jax.experimental.pallas import tpu as pltpu
from jax.sharding import PartitionSpec as P

MESH = pl.DeviceIdType.MESH
SIDE = 7
CELLS = SIDE * SIDE
HALF = 8
SLOTS = 2 * HALF
BODY = 48
ROWS = SLOTS * CELLS
KC = 1024
NC = 256


def dot(a, b):
    return jnp.dot(a, b, preferred_element_type=jnp.float32)


def kernel(
    comm,
    groups,
    planes,
    ti,
    tc,
    x_hbm,
    wr_hbm,
    sr,
    br,
    ws_hbm,
    ss,
    bs,
    we_hbm,
    se,
    be,
    out,
    x,
    wr,
    ws,
    we,
    xs,
    last,
    red,
    cin,
    acc,
    spat,
    tail,
    own,
    spill,
    arrived,
    cnt,
    got1,
    got2,
    got3,
    x_sem,
    wr_sem,
    ws_sem,
    we_sem,
    send1,
    recv1,
    send2,
    recv2,
    send3,
    recv3,
    spill_send,
    spill_recv,
):
    channels = x_hbm.shape[2]
    inner = wr_hbm.shape[1]
    chunks = channels // KC
    bf16 = jnp.bfloat16
    f32 = jnp.float32

    copies_x = []
    copies_r = []
    for k in range(chunks):
        at = pl.ds(k * KC, KC)
        cx = pltpu.make_async_copy(x_hbm.at[:, :, at], x[k], x_sem.at[k])
        cr = pltpu.make_async_copy(wr_hbm.at[at], wr.at[at], wr_sem.at[k])
        cx.start()
        cr.start()
        copies_x.append(cx)
        copies_r.append(cr)
    copies_s = {}
    for a in (1, 0, 2):
        cs = pltpu.make_async_copy(ws_hbm.at[a], ws.at[a], ws_sem.at[a])
        cs.start()
        copies_s[a] = cs
    ce = pltpu.make_async_copy(we_hbm, we, we_sem)
    ce.start()

    count = tc[0]
    if comm:
        g = lax.axis_index("grp")
        e = lax.axis_index("ext")
        ext = lax.axis_size("ext")
        plane = ext // planes
        p = e // plane
        q = lax.rem(e, plane)
        rank = g * ext + e
        total = groups * ext
        ahead = lax.rem(rank + 1, total)
        behind = lax.rem(rank + total - 1, total)

        def device(r):
            return (r // ext, lax.rem(r, ext))

        near = [lax.rem(q + k, plane) for k in range(1, plane)]
        far = [lax.rem(p + k, planes) for k in range(1, planes)]
        wide = [lax.rem(g + k, groups) for k in range(1, groups)]
        barrier = pltpu.get_barrier_semaphore()
        greeted = (
            [(g, p * plane + o) for o in near]
            + [(g, o * plane + q) for o in far]
            + [(o, e) for o in wide]
            + [device(behind)]
        )
        for who in greeted:
            pl.semaphore_signal(barrier, inc=1, device_id=who, device_id_type=MESH)

    def start(me, others, ids, where, box, send, recv):
        started = []
        for k, who in enumerate(ids):
            c = pltpu.make_async_remote_copy(
                src_ref=cnt.at[where],
                dst_ref=box.at[me],
                send_sem=send.at[k],
                recv_sem=recv.at[me],
                device_id=who,
                device_id_type=MESH,
            )
            c.start()
            started.append(c)
        return started

    def finish(me, others, ids, where, box, send, recv):
        before = jnp.zeros((1, 128), jnp.int32)
        whole = cnt[where]
        for k, (o, who) in enumerate(zip(others, ids)):
            pltpu.make_async_remote_copy(
                src_ref=cnt.at[where],
                dst_ref=box.at[o],
                send_sem=send.at[k],
                recv_sem=recv.at[o],
                device_id=who,
                device_id_type=MESH,
            ).wait()
            value = box[o]
            whole = whole + value
            before = before + jnp.where(o < me, value, 0)
        return before, whole

    slots = [jnp.clip(count - HALF + j, 0, SLOTS - 1) for j in range(HALF)]
    slots = slots + list(range(HALF))
    idx = [ti[0, s] for s in slots]

    for k in range(chunks):
        at = pl.ds(k * KC, KC)
        copies_x[k].wait()
        for s in range(SLOTS):
            xs[s * BODY : (s + 1) * BODY, at] = x[k][idx[s], 0:BODY, :]
            last[s : s + 1, at] = x[k][idx[s], BODY:CELLS, :].astype(f32)
        xs[SLOTS * BODY : ROWS, at] = last[:, at].astype(bf16)
        copies_r[k].wait()
        for m0, m1 in ((0, 256), (256, 512), (512, ROWS)):
            part = dot(xs[m0:m1, at], wr[at, :])
            if k > 0:
                part = part + acc[m0:m1]
            if k < chunks - 1:
                acc[m0:m1] = part
            else:
                red[m0:m1] = jnp.maximum(
                    part * sr[...][None, :] + br[...][None, :], 0.0
                ).astype(bf16)

    if comm:
        pl.semaphore_wait(barrier, len(greeted))
        cnt[0] = jnp.full((1, 128), count, jnp.int32)
        args1 = (q, near, [(g, p * plane + o) for o in near], 0, got1, send1, recv1)
        start(*args1)

    r = lax.broadcasted_iota(jnp.int32, (256, 256), 0)
    c = lax.broadcasted_iota(jnp.int32, (256, 256), 1)
    swap = jnp.where(
        (r // SLOTS == lax.rem(c, SLOTS)) & (lax.rem(r, SLOTS) == c // SLOTS), 1.0, 0.0
    ).astype(bf16)
    zero = jnp.zeros((SLOTS, inner), bf16)
    for i in range(SIDE):
        cin[i, 0] = zero
        cin[i, SIDE + 1] = zero
    for b in range(3):
        block = jnp.concatenate(
            [red[s * BODY + b * 16 : s * BODY + b * 16 + 16] for s in range(SLOTS)], axis=0
        )
        turned = dot(swap, block).astype(bf16)
        for t in range(16):
            cell = b * 16 + t
            cin[cell // SIDE, cell % SIDE + 1] = turned[t * SLOTS : (t + 1) * SLOTS]
    cin[SIDE - 1, SIDE] = red[SLOTS * BODY : ROWS]

    for a in (1, 0, 2):
        copies_s[a].wait()
        lo, hi = max(0, 1 - a), min(SIDE, SIDE + 1 - a)
        for i0, i1 in ((0, 2), (2, 4), (4, 7)):
            j0, j1 = max(i0, lo), min(i1, hi)
            m = (j1 - j0) * SIDE * SLOTS
            part = None
            for b in range(3):
                lhs = cin[j0 + a - 1 : j1 + a - 1, b : b + SIDE].reshape(m, inner)
                d = dot(lhs, ws[a, b])
                part = d if part is None else part + d
            o0, o1 = j0 * SIDE * SLOTS, j1 * SIDE * SLOTS
            if a == 1:
                acc[o0:o1] = part
            else:
                acc[o0:o1] = acc[o0:o1] + part
        if comm and a == 1:
            before1, whole1 = finish(*args1)
            cnt[1] = whole1
            args2 = (p, far, [(g, o * plane + q) for o in far], 1, got2, send2, recv2)
            start(*args2)
        if comm and a == 0:
            before2, whole2 = finish(*args2)
            cnt[2] = whole2
            args3 = (g, wide, [(o, e) for o in wide], 2, got3, send3, recv3)
            start(*args3)

    sp = lambda m0, m1: jnp.maximum(
        acc[m0:m1] * ss[...][None, :] + bs[...][None, :], 0.0
    ).astype(bf16)
    for b in range(3):
        turned = dot(swap, sp(b * 256, (b + 1) * 256)).astype(bf16)
        for s in range(SLOTS):
            spat[s * BODY + b * 16 : s * BODY + b * 16 + 16] = turned[s * 16 : s * 16 + 16]
    spat[SLOTS * BODY : ROWS] = sp(SLOTS * BODY, ROWS)

    ce.wait()

    def expanded(m0, m1, at):
        v = dot(spat[m0:m1], we[:, at]) * se[at][None, :] + be[at][None, :]
        return jnp.maximum(v + xs[m0:m1, at].astype(f32), 0.0)

    for half in range(2):
        for n in range(channels // NC):
            at = pl.ds(n * NC, NC)
            if half == 0:
                tail[:, at] = expanded(SLOTS * BODY, ROWS, at)
            v = expanded(half * HALF * BODY, (half + 1) * HALF * BODY, at)
            v = jnp.sum(v.reshape(HALF, BODY, NC), axis=1)
            v = (v + tail[half * HALF : (half + 1) * HALF, at]) * (1.0 / CELLS)
            if half == 0:
                spill[:, at] = v.astype(bf16)
            else:
                own[:, at] = v.astype(bf16)
        if half == 0 and comm:
            moved = pltpu.make_async_remote_copy(
                src_ref=spill,
                dst_ref=arrived,
                send_sem=spill_send,
                recv_sem=spill_recv,
                device_id=device(ahead),
                device_id_type=MESH,
            )
            moved.start()

    if comm:
        before3, _ = finish(*args3)
        backlog = before1 + before2 + before3 - rank * HALF
        moved.wait()
        prior = arrived[...]
    else:
        backlog = jnp.full((1, 128), 3, jnp.int32)
        prior = spill[...]
    both = jnp.concatenate([prior.astype(f32), own[...].astype(f32)], axis=0).astype(bf16)
    row = lax.broadcasted_iota(jnp.int32, (HALF, SLOTS), 0)
    col = lax.broadcasted_iota(jnp.int32, (HALF, SLOTS), 1)
    pick = jnp.where(col - row == HALF - backlog[:, :SLOTS], 1.0, 0.0).astype(bf16)
    out[...] = dot(pick, both).astype(bf16)


def on_device(comm, groups, planes, tiles, tissue_index, tissue_count, wr, sr, br, ws, ss, bs, we, se, be):
    cand, cells, channels = tiles.shape
    inner = wr.shape[1]
    plane = lax.axis_size("ext") // planes if comm else 8
    smem = pl.BlockSpec(memory_space=pltpu.SMEM)
    vmem = pl.BlockSpec(memory_space=pltpu.VMEM)
    hbm = pl.BlockSpec(memory_space=pl.ANY)
    bf16 = jnp.bfloat16
    f32 = jnp.float32
    dma = pltpu.SemaphoreType.DMA
    return pl.pallas_call(
        functools.partial(kernel, comm, groups, planes),
        out_shape=jax.ShapeDtypeStruct((HALF, channels), bf16),
        in_specs=[smem, smem, hbm, hbm, vmem, vmem, hbm, vmem, vmem, hbm, vmem, vmem],
        out_specs=vmem,
        scratch_shapes=[
            [pltpu.VMEM((cand, cells, KC), bf16)] * (channels // KC),
            pltpu.VMEM((channels, inner), bf16),
            pltpu.VMEM((3, 3, inner, inner), bf16),
            pltpu.VMEM((inner, channels), bf16),
            pltpu.VMEM((ROWS, channels), bf16),
            pltpu.VMEM((SLOTS, channels), f32),
            pltpu.VMEM((ROWS, inner), bf16),
            pltpu.VMEM((SIDE, SIDE + 2, SLOTS, inner), bf16),
            pltpu.VMEM((ROWS, inner), f32),
            pltpu.VMEM((ROWS, inner), bf16),
            pltpu.VMEM((SLOTS, channels), f32),
            pltpu.VMEM((HALF, channels), bf16),
            pltpu.VMEM((HALF, channels), bf16),
            pltpu.VMEM((HALF, channels), bf16),
            pltpu.VMEM((3, 1, 128), jnp.int32),
            pltpu.VMEM((plane, 1, 128), jnp.int32),
            pltpu.VMEM((planes, 1, 128), jnp.int32),
            pltpu.VMEM((groups, 1, 128), jnp.int32),
            dma((channels // KC,)),
            dma((channels // KC,)),
            dma((3,)),
            dma,
            dma((plane - 1,)),
            dma((plane,)),
            dma((planes - 1,)),
            dma((planes,)),
            dma((groups - 1,)),
            dma((groups,)),
            dma,
            dma,
        ],
        compiler_params=pltpu.CompilerParams(
            collective_id=0 if comm else None,
            has_side_effects=True,
            vmem_limit_bytes=56 * 1024 * 1024,
        ),
        name="bottleneck",
    )(tissue_index, tissue_count, tiles, wr, sr, br, ws, ss, bs, we, se, be)


def solution(mesh):
    axes = ("grp", "ext")
    split = P(axes)
    return jax.shard_map(
        functools.partial(on_device, True, mesh.shape["grp"], 8),
        mesh=mesh,
        in_specs=(split, split, split) + (P(),) * 9,
        out_specs=split,
        check_vma=False,
    )
```

```python
import functools

import jax
import jax.numpy as jnp
from jax import lax
from jax.experimental import pallas as pl
from jax.experimental.pallas import tpu as pltpu
from jax.sharding import PartitionSpec as P

MESH = pl.DeviceIdType.MESH
SIDE = 7
CELLS = SIDE * SIDE
HALF = 8
SLOTS = 2 * HALF
BODY = 48
ROWS = HALF * BODY
FULL = ROWS + HALF
FOLD = 4
KC = 1024
NC = 256
TEAM = 16
LANES = 128
bf16 = jnp.bfloat16
f32 = jnp.float32


def dot(a, b):
    return jnp.dot(a, b, preferred_element_type=jnp.float32)


class Exchange:
    def __init__(self, groups, cnt, got1, got2, send1, recv1, send2, recv2):
        self.cnt, self.boxes = cnt, (got1, got2)
        self.sends, self.recvs = (send1, send2), (recv1, recv2)
        g = lax.axis_index("grp")
        e = lax.axis_index("ext")
        ext = lax.axis_size("ext")
        per = ext // TEAM
        self.teams = groups * per
        self.rank = g * ext + e
        total = groups * ext
        self.device = lambda r: (r // ext, lax.rem(r, ext))
        team = self.rank // TEAM
        seat = lax.rem(self.rank, TEAM)
        seats = [lax.rem(seat + k, TEAM) for k in range(1, TEAM)]
        others = [lax.rem(team + k, self.teams) for k in range(1, self.teams)]
        self.me = (seat, team)
        self.peers = (seats, others)
        self.ids = (
            [self.device(team * TEAM + o) for o in seats],
            [self.device(o * TEAM + seat) for o in others],
        )
        self.ahead = self.device(lax.rem(self.rank + 1, total))
        behind = self.device(lax.rem(self.rank + total - 1, total))
        self.greeted = self.ids[0] + self.ids[1] + [behind]
        self.layer = lax.rem(e // (ext // 8), 8)

    def greet(self):
        barrier = pltpu.get_barrier_semaphore()
        for who in self.greeted:
            pl.semaphore_signal(barrier, inc=1, device_id=who, device_id_type=MESH)

    def enter(self):
        pl.semaphore_wait(pltpu.get_barrier_semaphore(), len(self.greeted))

    def start(self, stage):
        for k, who in enumerate(self.ids[stage]):
            pltpu.make_async_remote_copy(
                src_ref=self.cnt.at[stage],
                dst_ref=self.boxes[stage].at[self.me[stage]],
                send_sem=self.sends[stage].at[k],
                recv_sem=self.recvs[stage].at[self.me[stage]],
                device_id=who,
                device_id_type=MESH,
            ).start()

    def finish(self, stage):
        before = jnp.zeros((1, 128), jnp.int32)
        whole = self.cnt[stage]
        for k, (o, who) in enumerate(zip(self.peers[stage], self.ids[stage])):
            pltpu.make_async_remote_copy(
                src_ref=self.cnt.at[stage],
                dst_ref=self.boxes[stage].at[o],
                send_sem=self.sends[stage].at[k],
                recv_sem=self.recvs[stage].at[o],
                device_id=who,
                device_id_type=MESH,
            ).wait()
            value = self.boxes[stage][o]
            whole = whole + value
            before = before + jnp.where(o < self.me[stage], value, 0)
        return before, whole


def kernel(
    comm,
    groups,
    ti,
    tc,
    x_hbm,
    wr_hbm,
    sr,
    br,
    ws_hbm,
    ss,
    bs,
    we_hbm,
    se,
    be,
    out,
    x,
    wr,
    ws,
    we,
    xs,
    last,
    acc,
    flat,
    cin,
    spat,
    own,
    spill,
    arrived,
    cnt,
    base,
    got1,
    got2,
    x_sem,
    wr_sem,
    ws_sem,
    we_sem,
    send1,
    recv1,
    send2,
    recv2,
    spill_send,
    spill_recv,
):
    channels = x_hbm.shape[2]
    inner = wr_hbm.shape[1]
    chunks = channels // KC

    if comm:
        ex = Exchange(groups, cnt, got1, got2, send1, recv1, send2, recv2)
        ex.greet()

    copies_x = []
    copies_r = []
    for k in range(chunks):
        at = pl.ds(k * KC, KC)
        cx = pltpu.make_async_copy(x_hbm.at[:, :, at], x[k], x_sem.at[k])
        cr = pltpu.make_async_copy(wr_hbm.at[at], wr.at[at], wr_sem.at[k])
        cx.start()
        cr.start()
        copies_x.append(cx)
        copies_r.append(cr)
    copies_s = []
    for a in range(3):
        cs = pltpu.make_async_copy(ws_hbm.at[a], ws.at[a], ws_sem.at[a])
        cs.start()
        copies_s.append(cs)
    ce = pltpu.make_async_copy(we_hbm, we, we_sem)
    ce.start()

    count = tc[0]
    if comm:
        cnt[0] = jnp.full((1, 128), count, jnp.int32)

    def site(place):
        if not comm:
            return
        early, middle = ex.layer < 2, (ex.layer >= 2) & (ex.layer < 5)
        late = ex.layer >= 5
        first = {0: late, 2: middle, 4: early}
        second = {1: late, 3: middle, 5: early}
        if place in first:

            @pl.when(first[place])
            def _():
                ex.enter()
                ex.start(0)
                if place > 0:
                    send_spill()

        if place in second:

            @pl.when(second[place])
            def _():
                before, whole = ex.finish(0)
                base[...] = before
                cnt[1] = whole
                ex.start(1)

        if place == 2:

            @pl.when(late)
            def _():
                send_spill()

    def moved():
        return pltpu.make_async_remote_copy(
            src_ref=spill,
            dst_ref=arrived,
            send_sem=spill_send,
            recv_sem=spill_recv,
            device_id=ex.ahead,
            device_id_type=MESH,
        )

    def send_spill():
        moved().start()

    for half in range(2):
        if half == 0:
            slots = [jnp.clip(count - HALF + j, 0, SLOTS - 1) for j in range(HALF)]
        else:
            slots = list(range(HALF))
        idx = [ti[0, s] for s in slots]

        for k in range(chunks):
            at = pl.ds(k * KC, KC)
            if half == 0:
                copies_x[k].wait()
            for s in range(HALF):
                xs[half, s * BODY : (s + 1) * BODY, at] = x[k][idx[s], 0:BODY, :]
                last[s : s + 1, at] = x[k][idx[s], BODY:CELLS, :].astype(f32)
            xs[half, ROWS:FULL, at] = last[:, at].astype(bf16)
            if half == 0:
                copies_r[k].wait()
            part = dot(xs[half, :, at], wr[at, :])
            if k > 0:
                part = part + acc[0:FULL]
            if k < chunks - 1:
                acc[0:FULL] = part
            else:
                part = jnp.maximum(part * sr[...][None, :] + br[...][None, :], 0.0)
                for j in range(inner // LANES):
                    flat[j] = part[:, j * LANES : (j + 1) * LANES]
        site(3 * half)

        def cell(i, k):
            c = i * SIDE + k
            if i >= SIDE:
                return jnp.zeros((HALF, inner), f32)
            if c == BODY:
                parts = [flat[j, ROWS:FULL, :] for j in range(inner // LANES)]
            else:
                at = pl.ds(c, HALF, stride=BODY)
                parts = [flat[j, at, :] for j in range(inner // LANES)]
            return jnp.concatenate(parts, axis=1)

        none = jnp.zeros((HALF, inner), f32)
        if half == 0:
            for i in range(FOLD + 2):
                cin[i, 0] = jnp.zeros((SLOTS, inner), bf16)
                cin[i, SIDE + 1] = jnp.zeros((SLOTS, inner), bf16)
        for k in range(SIDE):
            for i in range(FOLD):
                low, high = cell(i, k), cell(i + FOLD, k)
                cin[i + 1, k + 1] = jnp.concatenate([low, high], axis=0).astype(bf16)
                if i == FOLD - 1:
                    cin[0, k + 1] = jnp.concatenate([none, low], axis=0).astype(bf16)
                if i == 0:
                    cin[FOLD + 1, k + 1] = jnp.concatenate([high, none], axis=0).astype(bf16)

        for a in range(3):
            if half == 0:
                copies_s[a].wait()
            lhs = jnp.concatenate(
                [
                    cin[a : a + FOLD, b : b + SIDE].reshape(FOLD * SIDE * SLOTS, inner)
                    for b in range(3)
                ],
                axis=1,
            )
            part = dot(lhs, ws[a].reshape(3 * inner, inner))
            if a > 0:
                part = part + acc[...]
            if a < 2:
                acc[...] = part
            else:
                part = jnp.maximum(part * ss[...][None, :] + bs[...][None, :], 0.0)
                for i in range(FOLD):
                    for k in range(SIDE):
                        v = (i * SIDE + k) * SLOTS
                        for up in range(2):
                            c = (i + up * FOLD) * SIDE + k
                            piece = part[v + up * HALF : v + up * HALF + HALF]
                            for j in range(inner // LANES):
                                strip = piece[:, j * LANES : (j + 1) * LANES]
                                if c < BODY:
                                    flat[j, pl.ds(c, HALF, stride=BODY), :] = strip
                                elif c == BODY:
                                    flat[j, ROWS:FULL, :] = strip
        for j in range(inner // LANES):
            spat[:, j * LANES : (j + 1) * LANES] = flat[j].astype(bf16)
        site(3 * half + 1)

        if half == 0:
            ce.wait()
        for n in range(channels // NC):
            at = pl.ds(n * NC, NC)
            v = dot(spat[...], we[:, at]) * se[at][None, :] + be[at][None, :]
            v = jnp.maximum(v + xs[half, :, at].astype(f32), 0.0)
            v = jnp.sum(v[:ROWS].reshape(HALF, BODY, NC), axis=1) + v[ROWS:FULL]
            v = (v * (1.0 / CELLS)).astype(bf16)
            if half == 0:
                spill[:, at] = v
            else:
                own[:, at] = v
        site(3 * half + 2)

    if comm:
        before, _ = ex.finish(1)
        backlog = base[...] + before - ex.rank * HALF
        moved().wait()
        prior = arrived[...]
    else:
        backlog = jnp.full((1, 128), 3, jnp.int32)
        prior = spill[...]
    both = jnp.concatenate([prior.astype(f32), own[...].astype(f32)], axis=0).astype(bf16)
    row = lax.broadcasted_iota(jnp.int32, (HALF, SLOTS), 0)
    col = lax.broadcasted_iota(jnp.int32, (HALF, SLOTS), 1)
    pick = jnp.where(col - row == HALF - backlog[:, :SLOTS], 1.0, 0.0).astype(bf16)
    out[...] = dot(pick, both).astype(bf16)


def on_device(comm, groups, tiles, tissue_index, tissue_count, wr, sr, br, ws, ss, bs, we, se, be):
    cand, cells, channels = tiles.shape
    inner = wr.shape[1]
    teams = groups * (lax.axis_size("ext") // TEAM) if comm else 16
    smem = pl.BlockSpec(memory_space=pltpu.SMEM)
    vmem = pl.BlockSpec(memory_space=pltpu.VMEM)
    hbm = pl.BlockSpec(memory_space=pl.ANY)
    dma = pltpu.SemaphoreType.DMA
    return pl.pallas_call(
        functools.partial(kernel, comm, groups),
        out_shape=jax.ShapeDtypeStruct((HALF, channels), bf16),
        in_specs=[smem, smem, hbm, hbm, vmem, vmem, hbm, vmem, vmem, hbm, vmem, vmem],
        out_specs=vmem,
        scratch_shapes=[
            [pltpu.VMEM((cand, cells, KC), bf16)] * (channels // KC),
            pltpu.VMEM((channels, inner), bf16),
            pltpu.VMEM((3, 3, inner, inner), bf16),
            pltpu.VMEM((inner, channels), bf16),
            pltpu.VMEM((2, FULL, channels), bf16),
            pltpu.VMEM((HALF, channels), f32),
            pltpu.VMEM((FOLD * SIDE * SLOTS, inner), f32),
            pltpu.VMEM((inner // LANES, FULL, LANES), f32),
            pltpu.VMEM((FOLD + 2, SIDE + 2, SLOTS, inner), bf16),
            pltpu.VMEM((FULL, inner), bf16),
            pltpu.VMEM((HALF, channels), bf16),
            pltpu.VMEM((HALF, channels), bf16),
            pltpu.VMEM((HALF, channels), bf16),
            pltpu.VMEM((2, 1, 128), jnp.int32),
            pltpu.VMEM((1, 128), jnp.int32),
            pltpu.VMEM((TEAM, 1, 128), jnp.int32),
            pltpu.VMEM((teams, 1, 128), jnp.int32),
            dma((channels // KC,)),
            dma((channels // KC,)),
            dma((3,)),
            dma,
            dma((TEAM - 1,)),
            dma((TEAM,)),
            dma((teams - 1,)),
            dma((teams,)),
            dma,
            dma,
        ],
        compiler_params=pltpu.CompilerParams(
            collective_id=0 if comm else None,
            has_side_effects=True,
            vmem_limit_bytes=56 * 1024 * 1024,
        ),
        name="bottleneck",
    )(tissue_index, tissue_count, tiles, wr, sr, br, ws, ss, bs, we, se, be)


def solution(mesh):
    axes = ("grp", "ext")
    split = P(axes)
    return jax.shard_map(
        functools.partial(on_device, True, mesh.shape["grp"]),
        mesh=mesh,
        in_specs=(split, split, split) + (P(),) * 9,
        out_specs=split,
        check_vma=False,
    )
```

```python
import functools

import jax
import jax.numpy as jnp
from jax import lax
from jax.experimental import pallas as pl
from jax.experimental.pallas import tpu as pltpu
from jax.sharding import PartitionSpec as P

MESH = pl.DeviceIdType.MESH
SIDE = 7
CELLS = SIDE * SIDE
HALF = 8
SLOTS = 2 * HALF
BODY = 48
ROWS = HALF * BODY
FULL = ROWS + HALF
FOLD = 4
KC = 1024
NC = 256
LAYERS = 8
ROW = 8
LANES = 128
bf16 = jnp.bfloat16
f32 = jnp.float32


def dot(a, b):
    return jnp.dot(a, b, preferred_element_type=jnp.float32)


class Exchange:
    def __init__(self, groups, cnt, box, table, tables, answer, sems):
        self.cnt, self.box, self.table, self.tables, self.answer = cnt, box, table, tables, answer
        self.post_send, self.post_recv, self.row_send, self.row_recv, self.out_send, self.out_recv = sems
        self.groups = groups
        g = self.g = lax.axis_index("grp")
        e = lax.axis_index("ext")
        ext = lax.axis_size("ext")
        self.z = e // ROW
        self.q = lax.rem(e, ROW)
        self.rank = g * ext + e
        total = groups * ext
        self.hub = self.z == 0
        after = lax.rem(self.rank + 1, total)
        before = lax.rem(self.rank + total - 1, total)
        self.ahead = (after // ext, lax.rem(after, ext))
        self.behind = (before // ext, lax.rem(before, ext))
        self.far = [lax.rem(g + k, groups) for k in range(groups)]
        self.mates = [lax.rem(self.q + k, ROW) for k in range(1, ROW)]

    def greet(self):
        barrier = pltpu.get_barrier_semaphore()

        def tell(who):
            pl.semaphore_signal(barrier, inc=1, device_id=who, device_id_type=MESH)

        @pl.when(self.hub)
        def _():
            for z in reversed(range(LAYERS)):
                for k, y in enumerate(self.far):
                    if z > 0 or k > 0:
                        tell((y, z * ROW + self.q))
            for o in self.mates:
                tell((self.g, o))

        @pl.when(jnp.logical_not(self.hub))
        def _():
            tell((self.g, self.q))

        tell(self.behind)

    def to_hub(self, k, y):
        mine = self.g * LAYERS + self.z
        return pltpu.make_async_remote_copy(
            src_ref=self.cnt,
            dst_ref=self.box.at[mine],
            send_sem=self.post_send.at[k],
            recv_sem=self.post_recv,
            device_id=(y, self.q),
            device_id_type=MESH,
        )

    def post(self, hub):
        barrier = pltpu.get_barrier_semaphore()
        if hub:
            pl.semaphore_wait(barrier, self.groups - 1 + ROW - 1 + LAYERS - 1 + 1)
        else:
            pl.semaphore_wait(barrier, self.groups + 1)
        for k, y in enumerate(self.far):
            if not hub or k > 0:
                self.to_hub(k, y).start()

    def sent(self, hub):
        for k, y in enumerate(self.far):
            if not hub or k > 0:
                self.to_hub(k, y).wait_send()

    def all_of(self, box, sem):
        rows = box.at[pl.ds(0, box.shape[0] - 1)]
        pltpu.make_async_copy(rows, rows, sem).wait()

    def collect(self):
        self.all_of(self.box, self.post_recv)
        self.box[self.g * LAYERS] = self.cnt[...]
        lower = jnp.zeros((1, 128), jnp.int32)
        for y in range(self.groups):
            plane = self.box[y * LAYERS]
            for z in range(1, LAYERS):
                plane = plane + self.box[y * LAYERS + z]
            lower = lower + jnp.where(y < self.g, plane, 0)
        for z in range(LAYERS):
            self.table[z] = self.box[self.g * LAYERS + z]
        self.table[LAYERS] = lower
        for k, o in enumerate(self.mates):
            self.to_mate(k, o).start()

    def to_mate(self, k, o):
        return pltpu.make_async_remote_copy(
            src_ref=self.table,
            dst_ref=self.tables.at[self.q],
            send_sem=self.row_send.at[k],
            recv_sem=self.row_recv,
            device_id=(self.g, o),
            device_id_type=MESH,
        )

    def to_plane(self, z):
        return pltpu.make_async_remote_copy(
            src_ref=self.answer.at[z],
            dst_ref=self.answer.at[0],
            send_sem=self.out_send.at[z - 1],
            recv_sem=self.out_recv,
            device_id=(self.g, z * ROW + self.q),
            device_id_type=MESH,
        )

    def settle(self):
        self.all_of(self.tables, self.row_recv)
        for k, o in enumerate(self.mates):
            self.to_mate(k, o).wait_send()
        self.tables[self.q] = self.table[...]
        whole = jnp.zeros((LAYERS + 1, 1, 128), jnp.int32)
        left = whole
        for o in range(ROW):
            value = self.tables[o]
            whole = whole + value
            left = left + jnp.where(o < self.q, value, 0)
        run = whole[LAYERS]
        for z in range(LAYERS):
            self.answer[z] = run + left[z]
            run = run + whole[z]
        for z in range(1, LAYERS):
            self.to_plane(z).start()
        self.sent(True)
        for z in range(1, LAYERS):
            self.to_plane(z).wait_send()

    def result(self):
        self.sent(False)
        self.to_plane(1).wait_recv()


def kernel(
    comm,
    groups,
    ti,
    tc,
    x_hbm,
    wr_hbm,
    sr,
    br,
    ws_hbm,
    ss,
    bs,
    we_hbm,
    se,
    be,
    out,
    x,
    wr,
    ws,
    we,
    xs,
    last,
    acc,
    flat,
    cin,
    spat,
    own,
    spill,
    arrived,
    cnt,
    box,
    table,
    tables,
    answer,
    x_sem,
    wr_sem,
    ws_sem,
    we_sem,
    sems,
    spill_send,
    spill_recv,
):
    channels = x_hbm.shape[2]
    inner = wr_hbm.shape[1]
    chunks = channels // KC

    if comm:
        ex = Exchange(groups, cnt, box, table, tables, answer, sems)
        ex.greet()

    copies_x = []
    copies_r = []
    for k in range(chunks):
        at = pl.ds(k * KC, KC)
        cx = pltpu.make_async_copy(x_hbm.at[:, :, at], x[k], x_sem.at[k])
        cr = pltpu.make_async_copy(wr_hbm.at[at], wr.at[at], wr_sem.at[k])
        cx.start()
        cr.start()
        copies_x.append(cx)
        copies_r.append(cr)
    copies_s = []
    for a in range(3):
        cs = pltpu.make_async_copy(ws_hbm.at[a], ws.at[a], ws_sem.at[a])
        cs.start()
        copies_s.append(cs)
    ce = pltpu.make_async_copy(we_hbm, we, we_sem)
    ce.start()

    count = tc[0]
    if comm:
        cnt[...] = jnp.full((1, 128), count, jnp.int32)

    def moved():
        return pltpu.make_async_remote_copy(
            src_ref=spill,
            dst_ref=arrived,
            send_sem=spill_send,
            recv_sem=spill_recv,
            device_id=ex.ahead,
            device_id_type=MESH,
        )

    def gather(half, k):
        if half == 0:
            slots = [jnp.clip(count - HALF + j, 0, SLOTS - 1) for j in range(HALF)]
        else:
            slots = list(range(HALF))
        at = pl.ds(k * KC, KC)
        for s, slot in enumerate(slots):
            tile = ti[0, slot]
            xs[half, s * BODY : (s + 1) * BODY, at] = x[k][tile, 0:BODY, :]
            last[s : s + 1, at] = x[k][tile, BODY:CELLS, :].astype(f32)
        xs[half, ROWS:FULL, at] = last[:, at].astype(bf16)

    def reduce(half, k):
        at = pl.ds(k * KC, KC)
        part = dot(xs[half, :, at], wr[at, :])
        if k > 0:
            part = part + flat_rows(half)
        if k == chunks - 1:
            part = jnp.maximum(part * sr[...][None, :] + br[...][None, :], 0.0)
        for j in range(inner // LANES):
            flat[half, j] = part[:, j * LANES : (j + 1) * LANES]

    def flat_rows(half):
        return jnp.concatenate([flat[half, j] for j in range(inner // LANES)], axis=1)

    def fold(half):
        none = jnp.zeros((HALF, inner), f32)

        def cell(i, k):
            c = i * SIDE + k
            if i >= SIDE:
                return none
            at = pl.ds(ROWS, HALF) if c == BODY else pl.ds(c, HALF, stride=BODY)
            return jnp.concatenate([flat[half, j, at, :] for j in range(inner // LANES)], axis=1)

        for k in range(SIDE):
            for i in range(FOLD):
                low, high = cell(i, k), cell(i + FOLD, k)
                cin[i + 1, k + 1] = jnp.concatenate([low, high], axis=0).astype(bf16)
                if i == FOLD - 1:
                    cin[0, k + 1] = jnp.concatenate([none, low], axis=0).astype(bf16)
                if i == 0:
                    cin[FOLD + 1, k + 1] = jnp.concatenate([high, none], axis=0).astype(bf16)

    def taps(half, a):
        lhs = jnp.concatenate(
            [
                cin[a : a + FOLD, b : b + SIDE].reshape(FOLD * SIDE * SLOTS, inner)
                for b in range(3)
            ],
            axis=1,
        )
        part = dot(lhs, ws[a].reshape(3 * inner, inner))
        if a > 0:
            part = part + acc[...]
        if a < 2:
            acc[...] = part
            return
        part = jnp.maximum(part * ss[...][None, :] + bs[...][None, :], 0.0)
        for i in range(FOLD):
            for k in range(SIDE):
                for up in range(2):
                    v = (i * SIDE + k) * SLOTS + up * HALF
                    c = (i + up * FOLD) * SIDE + k
                    if c > BODY:
                        continue
                    at = pl.ds(ROWS, HALF) if c == BODY else pl.ds(c, HALF, stride=BODY)
                    for j in range(inner // LANES):
                        flat[half, j, at, :] = part[v : v + HALF, j * LANES : (j + 1) * LANES]
        for j in range(inner // LANES):
            spat[:, j * LANES : (j + 1) * LANES] = flat[half, j].astype(bf16)

    def expand(half):
        for n in range(channels // NC):
            at = pl.ds(n * NC, NC)
            v = dot(spat[...], we[:, at]) * se[at][None, :] + be[at][None, :]
            v = jnp.maximum(v + xs[half, :, at].astype(f32), 0.0)
            v = jnp.sum(v[:ROWS].reshape(HALF, BODY, NC), axis=1) + v[ROWS:FULL]
            v = (v * (1.0 / CELLS)).astype(bf16)
            if half == 0:
                spill[:, at] = v
            else:
                own[:, at] = v

    for i in range(FOLD + 2):
        cin[i, 0] = jnp.zeros((SLOTS, inner), bf16)
        cin[i, SIDE + 1] = jnp.zeros((SLOTS, inner), bf16)
    for k in range(chunks):
        copies_x[k].wait()
        if comm and k == 0:

            @pl.when(ex.z >= LAYERS // 2)
            def _():
                ex.post(False)

        gather(0, k)
        gather(1, k)
        copies_r[k].wait()
        reduce(0, k)
        reduce(1, k)
        if comm and k == 0:

            @pl.when((ex.z > 0) & (ex.z < LAYERS // 2))
            def _():
                ex.post(False)

    fold(0)
    for a in range(3):
        copies_s[a].wait()
        taps(0, a)
    if comm:

        @pl.when(ex.hub)
        def _():
            ex.post(True)

    ce.wait()
    expand(0)
    if comm:
        moved().start()
    fold(1)
    for a in range(3):
        taps(1, a)
    if comm:

        @pl.when(ex.hub)
        def _():
            ex.collect()

    expand(1)

    if comm:

        @pl.when(ex.hub)
        def _():
            ex.settle()

        @pl.when(jnp.logical_not(ex.hub))
        def _():
            ex.result()

        backlog = answer[0] - ex.rank * HALF
        moved().wait()
        prior = arrived[...]
    else:
        backlog = jnp.full((1, 128), 3, jnp.int32)
        prior = spill[...]
    both = jnp.concatenate([prior.astype(f32), own[...].astype(f32)], axis=0).astype(bf16)
    row = lax.broadcasted_iota(jnp.int32, (HALF, SLOTS), 0)
    col = lax.broadcasted_iota(jnp.int32, (HALF, SLOTS), 1)
    pick = jnp.where(col - row == HALF - backlog[:, :SLOTS], 1.0, 0.0).astype(bf16)
    out[...] = dot(pick, both).astype(bf16)


def on_device(comm, groups, tiles, tissue_index, tissue_count, wr, sr, br, ws, ss, bs, we, se, be):
    cand, cells, channels = tiles.shape
    inner = wr.shape[1]
    smem = pl.BlockSpec(memory_space=pltpu.SMEM)
    vmem = pl.BlockSpec(memory_space=pltpu.VMEM)
    hbm = pl.BlockSpec(memory_space=pl.ANY)
    dma = pltpu.SemaphoreType.DMA
    return pl.pallas_call(
        functools.partial(kernel, comm, groups),
        out_shape=jax.ShapeDtypeStruct((HALF, channels), bf16),
        in_specs=[smem, smem, hbm, hbm, vmem, vmem, hbm, vmem, vmem, hbm, vmem, vmem],
        out_specs=vmem,
        scratch_shapes=[
            [pltpu.VMEM((cand, cells, KC), bf16)] * (channels // KC),
            pltpu.VMEM((channels, inner), bf16),
            pltpu.VMEM((3, 3, inner, inner), bf16),
            pltpu.VMEM((inner, channels), bf16),
            pltpu.VMEM((2, FULL, channels), bf16),
            pltpu.VMEM((HALF, channels), f32),
            pltpu.VMEM((FOLD * SIDE * SLOTS, inner), f32),
            pltpu.VMEM((2, inner // LANES, FULL, LANES), f32),
            pltpu.VMEM((FOLD + 2, SIDE + 2, SLOTS, inner), bf16),
            pltpu.VMEM((FULL, inner), bf16),
            pltpu.VMEM((HALF, channels), bf16),
            pltpu.VMEM((HALF, channels), bf16),
            pltpu.VMEM((HALF, channels), bf16),
            pltpu.VMEM((1, 128), jnp.int32),
            pltpu.VMEM((groups * LAYERS, 1, 128), jnp.int32),
            pltpu.VMEM((LAYERS + 1, 1, 128), jnp.int32),
            pltpu.VMEM((ROW, LAYERS + 1, 1, 128), jnp.int32),
            pltpu.VMEM((LAYERS, 1, 128), jnp.int32),
            dma((channels // KC,)),
            dma((channels // KC,)),
            dma((3,)),
            dma,
            [
                dma((groups,)),
                dma,
                dma((ROW - 1,)),
                dma,
                dma((LAYERS - 1,)),
                dma,
            ],
            dma,
            dma,
        ],
        compiler_params=pltpu.CompilerParams(
            collective_id=0 if comm else None,
            has_side_effects=True,
            vmem_limit_bytes=56 * 1024 * 1024,
        ),
        name="bottleneck",
    )(tissue_index, tissue_count, tiles, wr, sr, br, ws, ss, bs, we, se, be)


def solution(mesh):
    axes = ("grp", "ext")
    split = P(axes)
    return jax.shard_map(
        functools.partial(on_device, True, mesh.shape["grp"]),
        mesh=mesh,
        in_specs=(split, split, split) + (P(),) * 9,
        out_specs=split,
        check_vma=False,
    )
```

```python
import functools

import jax
import jax.numpy as jnp
from jax import lax
from jax.experimental import pallas as pl
from jax.experimental.pallas import tpu as pltpu
from jax.sharding import PartitionSpec as P

MESH = pl.DeviceIdType.MESH
SIDE = 7
CELLS = SIDE * SIDE
HALF = 8
SLOTS = 2 * HALF
BODY = 48
ROWS = HALF * BODY
FULL = ROWS + HALF
FOLD = 4
KC = 512
NC = 256
LAYERS = 8
AHEAD = 4
ROW = 8
LANES = 128
bf16 = jnp.bfloat16
f32 = jnp.float32


def dot(a, b):
    return jnp.dot(a, b, preferred_element_type=jnp.float32)


class Exchange:
    def __init__(self, groups, cnt, box, table, tables, answer, sems):
        self.cnt, self.box, self.table, self.tables, self.answer = cnt, box, table, tables, answer
        self.post_send, self.post_recv, self.row_send, self.row_recv, self.out_send, self.out_recv = sems
        self.groups = groups
        g = self.g = lax.axis_index("grp")
        e = lax.axis_index("ext")
        ext = lax.axis_size("ext")
        self.z = e // ROW
        self.q = lax.rem(e, ROW)
        self.rank = g * ext + e
        total = groups * ext
        self.hub = self.z == 0
        after = lax.rem(self.rank + 1, total)
        before = lax.rem(self.rank + total - 1, total)
        self.ahead = (after // ext, lax.rem(after, ext))
        self.behind = (before // ext, lax.rem(before, ext))
        self.far = [lax.rem(g + k, groups) for k in range(groups)]
        self.mates = [lax.rem(self.q + k, ROW) for k in range(1, ROW)]

    def greet(self):
        barrier = pltpu.get_barrier_semaphore()

        def tell(who):
            pl.semaphore_signal(barrier, inc=1, device_id=who, device_id_type=MESH)

        @pl.when(self.hub)
        def _():
            for z in reversed(range(LAYERS)):
                for k, y in enumerate(self.far):
                    if z > 0 or k > 0:
                        tell((y, z * ROW + self.q))
            for o in self.mates:
                tell((self.g, o))

        @pl.when(jnp.logical_not(self.hub))
        def _():
            tell((self.g, self.q))

        tell(self.behind)

    def to_hub(self, k, y):
        mine = self.g * LAYERS + self.z
        return pltpu.make_async_remote_copy(
            src_ref=self.cnt,
            dst_ref=self.box.at[mine],
            send_sem=self.post_send.at[k],
            recv_sem=self.post_recv,
            device_id=(y, self.q),
            device_id_type=MESH,
        )

    def post(self, hub):
        barrier = pltpu.get_barrier_semaphore()
        if hub:
            pl.semaphore_wait(barrier, self.groups - 1 + ROW - 1 + LAYERS - 1 + 1)
        else:
            pl.semaphore_wait(barrier, self.groups + 1)
        for k, y in enumerate(self.far):
            if not hub or k > 0:
                self.to_hub(k, y).start()

    def sent(self, hub):
        for k, y in enumerate(self.far):
            if not hub or k > 0:
                self.to_hub(k, y).wait_send()

    def all_of(self, box, sem):
        rows = box.at[pl.ds(0, box.shape[0] - 1)]
        pltpu.make_async_copy(rows, rows, sem).wait()

    def collect(self):
        self.all_of(self.box, self.post_recv)
        self.box[self.g * LAYERS] = self.cnt[...]
        lane = lax.broadcasted_iota(jnp.int32, (1, 128), 1)
        lower = jnp.zeros((1, 128), jnp.int32)
        for y in range(self.groups):
            plane = self.box[y * LAYERS]
            for z in range(1, LAYERS):
                plane = plane + self.box[y * LAYERS + z]
            lower = lower + jnp.where(y < self.g, plane, 0)
        table = jnp.where(lane == LAYERS, lower, 0)
        for z in range(LAYERS):
            table = jnp.where(lane == z, self.box[self.g * LAYERS + z], table)
        self.table[...] = table
        for k, o in enumerate(self.mates):
            self.to_mate(k, o).start()

    def to_mate(self, k, o):
        return pltpu.make_async_remote_copy(
            src_ref=self.table,
            dst_ref=self.tables.at[self.q],
            send_sem=self.row_send.at[k],
            recv_sem=self.row_recv,
            device_id=(self.g, o),
            device_id_type=MESH,
        )

    def to_plane(self, z):
        return pltpu.make_async_remote_copy(
            src_ref=self.answer,
            dst_ref=self.answer,
            send_sem=self.out_send.at[z - 1],
            recv_sem=self.out_recv,
            device_id=(self.g, z * ROW + self.q),
            device_id_type=MESH,
        )

    def settle(self):
        self.all_of(self.tables, self.row_recv)
        mine = self.table[...]
        whole = mine
        left = jnp.zeros((1, 128), jnp.int32)
        for o in range(ROW):
            value = jnp.where(o == self.q, 0, self.tables[o])
            whole = whole + value
            left = left + jnp.where(o < self.q, value, 0)
        self.answer[0] = whole
        self.answer[1] = left
        for z in range(1, LAYERS):
            self.to_plane(z).start()

    def result(self):
        self.to_plane(1).wait_recv()

    def offset(self):
        lane = lax.broadcasted_iota(jnp.int32, (1, 128), 1)
        take = jnp.where((lane < self.z) | (lane == LAYERS), self.answer[0], 0)
        take = take + jnp.where(lane == self.z, self.answer[1], 0)
        return jnp.sum(take, axis=1, keepdims=True)

    def close(self, hub):
        self.sent(hub)
        if hub:
            for k, o in enumerate(self.mates):
                self.to_mate(k, o).wait_send()
            for z in range(1, LAYERS):
                self.to_plane(z).wait_send()


def kernel(
    comm,
    groups,
    ti_hbm,
    tc_hbm,
    x_hbm,
    wr_hbm,
    sr_hbm,
    br_hbm,
    ws_hbm,
    ss_hbm,
    bs_hbm,
    we_hbm,
    se_hbm,
    be_hbm,
    out,
    small,
    x,
    wr,
    ws,
    we,
    xs,
    last,
    acc,
    flat,
    cin,
    spat,
    own,
    spill,
    arrived,
    cnt,
    box,
    table,
    tables,
    answer,
    small_sem,
    x_sem,
    wr_sem,
    ws_sem,
    we_sem,
    sems,
    spill_send,
    spill_recv,
):
    channels = x_hbm.shape[2]
    inner = wr_hbm.shape[1]
    chunks = channels // KC

    if comm:
        ex = Exchange(groups, cnt, box, table, tables, answer, sems)

    ti, tc, sr, br, ss, bs, se, be = small
    fetched = [
        pltpu.make_async_copy(a, b, small_sem.at[n])
        for n, (a, b) in enumerate(
            zip((ti_hbm, tc_hbm, sr_hbm, br_hbm, ss_hbm, bs_hbm, se_hbm, be_hbm), small)
        )
    ]
    units = []
    for k in range(chunks):
        at = pl.ds(k * KC, KC)
        units.append(
            [
                pltpu.make_async_copy(x_hbm.at[:, :, at], x[k], x_sem.at[k]),
                pltpu.make_async_copy(wr_hbm.at[at], wr.at[at], wr_sem.at[k]),
            ]
        )
    for a in range(3):
        units.append([pltpu.make_async_copy(ws_hbm.at[a], ws.at[a], ws_sem.at[a])])
    units.append([pltpu.make_async_copy(we_hbm, we, we_sem)])

    def begin(n):
        if n < len(units):
            for c in units[n]:
                c.start()

    def ready(n):
        for c in units[n]:
            c.wait()
        begin(n + AHEAD)

    for c in fetched[:2]:
        c.start()
    for n in range(AHEAD):
        begin(n)
    for c in fetched[2:]:
        c.start()
    if comm:
        ex.greet()
    for c in fetched[:2]:
        c.wait()

    count = tc[0]
    if comm:
        cnt[...] = jnp.full((1, 128), count, jnp.int32)

    def moved():
        return pltpu.make_async_remote_copy(
            src_ref=spill,
            dst_ref=arrived,
            send_sem=spill_send,
            recv_sem=spill_recv,
            device_id=ex.ahead,
            device_id_type=MESH,
        )

    def gather(half, k):
        if half == 0:
            slots = [jnp.clip(count - HALF + j, 0, SLOTS - 1) for j in range(HALF)]
        else:
            slots = list(range(HALF))
        at = pl.ds(k * KC, KC)
        for s, slot in enumerate(slots):
            tile = ti[0, slot]
            xs[half, s * BODY : (s + 1) * BODY, at] = x[k][tile, 0:BODY, :]
            last[s : s + 1, at] = x[k][tile, BODY:CELLS, :].astype(f32)
        xs[half, ROWS:FULL, at] = last[:, at].astype(bf16)

    def reduce(half, k):
        at = pl.ds(k * KC, KC)
        part = dot(xs[half, :, at], wr[at, :])
        if k > 0:
            part = part + flat_rows(half)
        if k == chunks - 1:
            part = jnp.maximum(part * sr[...][None, :] + br[...][None, :], 0.0)
        for j in range(inner // LANES):
            flat[half, j] = part[:, j * LANES : (j + 1) * LANES]

    def flat_rows(half):
        return jnp.concatenate([flat[half, j] for j in range(inner // LANES)], axis=1)

    def fold(half):
        none = jnp.zeros((HALF, inner), f32)

        def cell(i, k):
            c = i * SIDE + k
            if i >= SIDE:
                return none
            at = pl.ds(ROWS, HALF) if c == BODY else pl.ds(c, HALF, stride=BODY)
            return jnp.concatenate([flat[half, j, at, :] for j in range(inner // LANES)], axis=1)

        for k in range(SIDE):
            for i in range(FOLD):
                low, high = cell(i, k), cell(i + FOLD, k)
                cin[i + 1, k + 1] = jnp.concatenate([low, high], axis=0).astype(bf16)
                if i == FOLD - 1:
                    cin[0, k + 1] = jnp.concatenate([none, low], axis=0).astype(bf16)
                if i == 0:
                    cin[FOLD + 1, k + 1] = jnp.concatenate([high, none], axis=0).astype(bf16)

    def taps(half, a):
        lhs = jnp.concatenate(
            [
                cin[a : a + FOLD, b : b + SIDE].reshape(FOLD * SIDE * SLOTS, inner)
                for b in range(3)
            ],
            axis=1,
        )
        part = dot(lhs, ws[a].reshape(3 * inner, inner))
        if a > 0:
            part = part + acc[...]
        if a < 2:
            acc[...] = part
            return
        part = jnp.maximum(part * ss[...][None, :] + bs[...][None, :], 0.0)
        for i in range(FOLD):
            for k in range(SIDE):
                for up in range(2):
                    v = (i * SIDE + k) * SLOTS + up * HALF
                    c = (i + up * FOLD) * SIDE + k
                    if c > BODY:
                        continue
                    at = pl.ds(ROWS, HALF) if c == BODY else pl.ds(c, HALF, stride=BODY)
                    for j in range(inner // LANES):
                        flat[half, j, at, :] = part[v : v + HALF, j * LANES : (j + 1) * LANES]
        for j in range(inner // LANES):
            spat[:, j * LANES : (j + 1) * LANES] = flat[half, j].astype(bf16)

    def expand(half):
        for n in range(channels // NC):
            at = pl.ds(n * NC, NC)
            v = dot(spat[...], we[:, at]) * se[at][None, :] + be[at][None, :]
            v = jnp.maximum(v + xs[half, :, at].astype(f32), 0.0)
            v = jnp.sum(v[:ROWS].reshape(HALF, BODY, NC), axis=1) + v[ROWS:FULL]
            v = (v * (1.0 / CELLS)).astype(bf16)
            if half == 0:
                spill[:, at] = v
            else:
                own[:, at] = v

    for i in range(FOLD + 2):
        cin[i, 0] = jnp.zeros((SLOTS, inner), bf16)
        cin[i, SIDE + 1] = jnp.zeros((SLOTS, inner), bf16)
    if comm:

        @pl.when(ex.z >= LAYERS // 2)
        def _():
            ex.post(False)

    for k in range(chunks):
        ready(k)
        gather(0, k)
        gather(1, k)
        if k == chunks - 1:
            for c in fetched[2:]:
                c.wait()
        reduce(0, k)
        reduce(1, k)
        if comm and k == 0:

            @pl.when((ex.z > 0) & (ex.z < LAYERS // 2))
            def _():
                ex.post(False)

    fold(0)
    for a in range(3):
        ready(chunks + a)
        taps(0, a)
    if comm:

        @pl.when(ex.hub)
        def _():
            ex.post(True)

    ready(chunks + 3)
    expand(0)
    if comm:
        moved().start()
    fold(1)
    for a in range(3):
        taps(1, a)
    expand(1)

    if comm:

        @pl.when(ex.hub)
        def _():
            ex.collect()
            ex.settle()

        @pl.when(jnp.logical_not(ex.hub))
        def _():
            ex.result()

        backlog = ex.offset() - ex.rank * HALF
        moved().wait_recv()
        prior = arrived[...]
    else:
        backlog = jnp.full((1, 1), 3, jnp.int32)
        prior = spill[...]
    both = jnp.concatenate([prior.astype(f32), own[...].astype(f32)], axis=0).astype(bf16)
    row = lax.broadcasted_iota(jnp.int32, (HALF, SLOTS), 0)
    col = lax.broadcasted_iota(jnp.int32, (HALF, SLOTS), 1)
    pick = jnp.where(col - row == HALF - backlog, 1.0, 0.0).astype(bf16)
    out[...] = dot(pick, both).astype(bf16)
    if comm:
        moved().wait_send()

        @pl.when(ex.hub)
        def _():
            ex.close(True)

        @pl.when(jnp.logical_not(ex.hub))
        def _():
            ex.close(False)


def on_device(comm, groups, tiles, tissue_index, tissue_count, wr, sr, br, ws, ss, bs, we, se, be):
    cand, cells, channels = tiles.shape
    inner = wr.shape[1]
    vmem = pl.BlockSpec(memory_space=pltpu.VMEM)
    hbm = pl.BlockSpec(memory_space=pl.ANY)
    dma = pltpu.SemaphoreType.DMA
    return pl.pallas_call(
        functools.partial(kernel, comm, groups),
        out_shape=jax.ShapeDtypeStruct((HALF, channels), bf16),
        in_specs=[hbm] * 12,
        out_specs=vmem,
        scratch_shapes=[
            [
                pltpu.SMEM((1, cand), jnp.int32),
                pltpu.SMEM((1,), jnp.int32),
            ]
            + [pltpu.VMEM((inner,), f32)] * 4
            + [pltpu.VMEM((channels,), f32)] * 2,
            [pltpu.VMEM((cand, cells, KC), bf16)] * (channels // KC),
            pltpu.VMEM((channels, inner), bf16),
            pltpu.VMEM((3, 3, inner, inner), bf16),
            pltpu.VMEM((inner, channels), bf16),
            pltpu.VMEM((2, FULL, channels), bf16),
            pltpu.VMEM((HALF, channels), f32),
            pltpu.VMEM((FOLD * SIDE * SLOTS, inner), f32),
            pltpu.VMEM((2, inner // LANES, FULL, LANES), f32),
            pltpu.VMEM((FOLD + 2, SIDE + 2, SLOTS, inner), bf16),
            pltpu.VMEM((FULL, inner), bf16),
            pltpu.VMEM((HALF, channels), bf16),
            pltpu.VMEM((HALF, channels), bf16),
            pltpu.VMEM((HALF, channels), bf16),
            pltpu.VMEM((1, 128), jnp.int32),
            pltpu.VMEM((groups * LAYERS, 1, 128), jnp.int32),
            pltpu.VMEM((1, 128), jnp.int32),
            pltpu.VMEM((ROW, 1, 128), jnp.int32),
            pltpu.VMEM((2, 1, 128), jnp.int32),
            dma((8,)),
            dma((channels // KC,)),
            dma((channels // KC,)),
            dma((3,)),
            dma,
            [
                dma((groups,)),
                dma,
                dma((ROW - 1,)),
                dma,
                dma((LAYERS - 1,)),
                dma,
            ],
            dma,
            dma,
        ],
        compiler_params=pltpu.CompilerParams(
            collective_id=0 if comm else None,
            has_side_effects=True,
            vmem_limit_bytes=56 * 1024 * 1024,
        ),
        name="bottleneck",
    )(tissue_index, tissue_count, tiles, wr, sr, br, ws, ss, bs, we, se, be)


def solution(mesh):
    axes = ("grp", "ext")
    split = P(axes)
    return jax.shard_map(
        functools.partial(on_device, True, mesh.shape["grp"]),
        mesh=mesh,
        in_specs=(split, split, split) + (P(),) * 9,
        out_specs=split,
        check_vma=False,
    )
```

```python
import functools

import jax
import jax.numpy as jnp
from jax import lax
from jax.experimental import pallas as pl
from jax.experimental.pallas import tpu as pltpu
from jax.sharding import PartitionSpec as P

MESH = pl.DeviceIdType.MESH
SIDE = 7
CELLS = SIDE * SIDE
HALF = 8
SLOTS = 2 * HALF
BODY = 48
ROWS = HALF * BODY
FULL = ROWS + HALF
FOLD = 4
KC = 512
NC = 256
LAYERS = 8
AHEAD = 4
ROW = 8
LANES = 128
bf16 = jnp.bfloat16
f32 = jnp.float32


def dot(a, b):
    return jnp.dot(a, b, preferred_element_type=jnp.float32)


class Exchange:
    def __init__(self, groups, cnt, box, table, tables, answer, sems):
        self.cnt, self.box, self.table, self.tables, self.answer = cnt, box, table, tables, answer
        self.post_send, self.post_recv, self.row_send, self.row_recv, self.out_send, self.out_recv = sems
        self.groups = groups
        g = self.g = lax.axis_index("grp")
        e = lax.axis_index("ext")
        ext = lax.axis_size("ext")
        self.z = e // ROW
        self.q = lax.rem(e, ROW)
        self.rank = g * ext + e
        total = self.total = groups * ext
        self.hub = self.z == 0
        after = lax.rem(self.rank + 1, total)
        before = lax.rem(self.rank + total - 1, total)
        self.ahead = (after // ext, lax.rem(after, ext))
        self.behind = (before // ext, lax.rem(before, ext))
        self.mates = [lax.rem(self.q + k, ROW) for k in range(1, ROW)]

    def greet(self):
        barrier = pltpu.get_barrier_semaphore()

        def tell(who):
            pl.semaphore_signal(barrier, inc=1, device_id=who, device_id_type=MESH)

        @pl.when(self.hub)
        def _():
            for y in reversed(range(self.groups)):

                @pl.when(y < self.g)
                def _():
                    tell((y, self.q))

                @pl.when(y <= self.g)
                def _():
                    for z in reversed(range(1, LAYERS)):
                        tell((y, z * ROW + self.q))

            for o in self.mates:
                tell((self.g, o))

        @pl.when(jnp.logical_not(self.hub))
        def _():
            tell((self.g, self.q))

        tell(self.behind)

    def to_hub(self, y):
        return pltpu.make_async_remote_copy(
            src_ref=self.cnt,
            dst_ref=self.box.at[self.g * LAYERS + self.z],
            send_sem=self.post_send.at[y],
            recv_sem=self.post_recv,
            device_id=(y, self.q),
            device_id_type=MESH,
        )

    def each_hub(self, hub, act):
        for y in range(self.groups):

            @pl.when(y > self.g if hub else y >= self.g)
            def _():
                act(self.to_hub(y))

    def post(self, hub):
        own = ROW - 1 + LAYERS - 1 if hub else 1
        pl.semaphore_wait(pltpu.get_barrier_semaphore(), self.groups - 1 - self.g + own + 1)
        self.each_hub(hub, lambda c: c.start())

    def sent(self, hub):
        self.each_hub(hub, lambda c: c.wait_send())

    def all_of(self, box, count, sem):
        rows = box.at[pl.ds(0, count - 1)]
        pltpu.make_async_copy(rows, rows, sem).wait()

    def collect(self):
        for y in range(self.groups):

            @pl.when(y == self.g)
            def _():
                self.all_of(self.box, (y + 1) * LAYERS, self.post_recv)

        self.box[self.g * LAYERS] = self.cnt[...]
        lane = lax.broadcasted_iota(jnp.int32, (1, 128), 1)
        lower = jnp.zeros((1, 128), jnp.int32)
        for y in range(self.groups - 1):
            plane = self.box[y * LAYERS]
            for z in range(1, LAYERS):
                plane = plane + self.box[y * LAYERS + z]
            lower = lower + jnp.where(y < self.g, plane, 0)
        table = jnp.where(lane == LAYERS, lower, 0)
        for z in range(LAYERS):
            table = jnp.where(lane == z, self.box[self.g * LAYERS + z], table)
        self.table[...] = table
        for k, o in enumerate(self.mates):
            self.to_mate(k, o).start()

    def to_mate(self, k, o):
        return pltpu.make_async_remote_copy(
            src_ref=self.table,
            dst_ref=self.tables.at[self.q],
            send_sem=self.row_send.at[k],
            recv_sem=self.row_recv,
            device_id=(self.g, o),
            device_id_type=MESH,
        )

    def to_plane(self, z):
        return pltpu.make_async_remote_copy(
            src_ref=self.answer,
            dst_ref=self.answer,
            send_sem=self.out_send.at[z - 1],
            recv_sem=self.out_recv,
            device_id=(self.g, z * ROW + self.q),
            device_id_type=MESH,
        )

    def settle(self):
        self.all_of(self.tables, ROW, self.row_recv)
        mine = self.table[...]
        whole = mine
        left = jnp.zeros((1, 128), jnp.int32)
        for o in range(ROW):
            value = jnp.where(o == self.q, 0, self.tables[o])
            whole = whole + value
            left = left + jnp.where(o < self.q, value, 0)
        self.answer[0] = whole
        self.answer[1] = left
        for z in range(1, LAYERS):
            self.to_plane(z).start()

    def result(self):
        self.to_plane(1).wait_recv()

    def offset(self):
        lane = lax.broadcasted_iota(jnp.int32, (1, 128), 1)
        take = jnp.where((lane < self.z) | (lane == LAYERS), self.answer[0], 0)
        take = take + jnp.where(lane == self.z, self.answer[1], 0)
        return jnp.sum(take, axis=1, keepdims=True)

    def close(self, hub):
        self.sent(hub)
        if hub:
            for k, o in enumerate(self.mates):
                self.to_mate(k, o).wait_send()
            for z in range(1, LAYERS):
                self.to_plane(z).wait_send()


def kernel(
    comm,
    groups,
    ti_hbm,
    tc_hbm,
    x_hbm,
    wr_hbm,
    sr_hbm,
    br_hbm,
    ws_hbm,
    ss_hbm,
    bs_hbm,
    we_hbm,
    se_hbm,
    be_hbm,
    out,
    small,
    x,
    wr,
    ws,
    we,
    xs,
    last,
    acc,
    flat,
    cin,
    spat,
    own,
    spill,
    arrived,
    cnt,
    box,
    table,
    tables,
    answer,
    small_sem,
    x_sem,
    wr_sem,
    ws_sem,
    we_sem,
    sems,
    spill_send,
    spill_recv,
):
    channels = x_hbm.shape[2]
    inner = wr_hbm.shape[1]
    chunks = channels // KC

    if comm:
        ex = Exchange(groups, cnt, box, table, tables, answer, sems)

    ti, tc, sr, br, ss, bs, se, be = small
    fetched = [
        pltpu.make_async_copy(a, b, small_sem.at[n])
        for n, (a, b) in enumerate(
            zip((ti_hbm, tc_hbm, sr_hbm, br_hbm, ss_hbm, bs_hbm, se_hbm, be_hbm), small)
        )
    ]
    units = []
    for k in range(chunks):
        at = pl.ds(k * KC, KC)
        units.append(
            [
                pltpu.make_async_copy(x_hbm.at[:, :, at], x[k], x_sem.at[k]),
                pltpu.make_async_copy(wr_hbm.at[at], wr.at[at], wr_sem.at[k]),
            ]
        )
    for a in range(3):
        units.append([pltpu.make_async_copy(ws_hbm.at[a], ws.at[a], ws_sem.at[a])])
    units.append([pltpu.make_async_copy(we_hbm, we, we_sem)])

    def begin(n):
        if n < len(units):
            for c in units[n]:
                c.start()

    def ready(n):
        for c in units[n]:
            c.wait()
        begin(n + AHEAD)

    for c in fetched[:2]:
        c.start()
    for n in range(AHEAD):
        begin(n)
    for c in fetched[2:]:
        c.start()
    if comm:
        ex.greet()
    for c in fetched[:2]:
        c.wait()

    count = tc[0]
    if comm:
        cnt[...] = jnp.full((1, 128), count, jnp.int32)

    def moved():
        return pltpu.make_async_remote_copy(
            src_ref=spill,
            dst_ref=arrived,
            send_sem=spill_send,
            recv_sem=spill_recv,
            device_id=ex.ahead,
            device_id_type=MESH,
        )

    def gather(half, k):
        if half == 0:
            slots = [jnp.clip(count - HALF + j, 0, SLOTS - 1) for j in range(HALF)]
        else:
            slots = list(range(HALF))
        at = pl.ds(k * KC, KC)
        for s, slot in enumerate(slots):
            tile = ti[0, slot]
            xs[half, s * BODY : (s + 1) * BODY, at] = x[k][tile, 0:BODY, :]
            last[s : s + 1, at] = x[k][tile, BODY:CELLS, :].astype(f32)
        xs[half, ROWS:FULL, at] = last[:, at].astype(bf16)

    def reduce(half, k):
        at = pl.ds(k * KC, KC)
        part = dot(xs[half, :, at], wr[at, :])
        if k > 0:
            part = part + flat_rows(half)
        if k == chunks - 1:
            part = jnp.maximum(part * sr[...][None, :] + br[...][None, :], 0.0)
        for j in range(inner // LANES):
            flat[half, j] = part[:, j * LANES : (j + 1) * LANES]

    def flat_rows(half):
        return jnp.concatenate([flat[half, j] for j in range(inner // LANES)], axis=1)

    def fold(half):
        none = jnp.zeros((HALF, inner), f32)

        def cell(i, k):
            c = i * SIDE + k
            if i >= SIDE:
                return none
            at = pl.ds(ROWS, HALF) if c == BODY else pl.ds(c, HALF, stride=BODY)
            return jnp.concatenate([flat[half, j, at, :] for j in range(inner // LANES)], axis=1)

        for k in range(SIDE):
            for i in range(FOLD):
                low, high = cell(i, k), cell(i + FOLD, k)
                cin[i + 1, k + 1] = jnp.concatenate([low, high], axis=0).astype(bf16)
                if i == FOLD - 1:
                    cin[0, k + 1] = jnp.concatenate([none, low], axis=0).astype(bf16)
                if i == 0:
                    cin[FOLD + 1, k + 1] = jnp.concatenate([high, none], axis=0).astype(bf16)

    def taps(half, a):
        lhs = jnp.concatenate(
            [
                cin[a : a + FOLD, b : b + SIDE].reshape(FOLD * SIDE * SLOTS, inner)
                for b in range(3)
            ],
            axis=1,
        )
        part = dot(lhs, ws[a].reshape(3 * inner, inner))
        if a > 0:
            part = part + acc[...]
        if a < 2:
            acc[...] = part
            return
        part = jnp.maximum(part * ss[...][None, :] + bs[...][None, :], 0.0)
        for i in range(FOLD):
            for k in range(SIDE):
                for up in range(2):
                    v = (i * SIDE + k) * SLOTS + up * HALF
                    c = (i + up * FOLD) * SIDE + k
                    if c > BODY:
                        continue
                    at = pl.ds(ROWS, HALF) if c == BODY else pl.ds(c, HALF, stride=BODY)
                    for j in range(inner // LANES):
                        flat[half, j, at, :] = part[v : v + HALF, j * LANES : (j + 1) * LANES]
        for j in range(inner // LANES):
            spat[:, j * LANES : (j + 1) * LANES] = flat[half, j].astype(bf16)

    def expand(half):
        for n in range(channels // NC):
            at = pl.ds(n * NC, NC)
            v = dot(spat[...], we[:, at]) * se[at][None, :] + be[at][None, :]
            v = jnp.maximum(v + xs[half, :, at].astype(f32), 0.0)
            v = jnp.sum(v[:ROWS].reshape(HALF, BODY, NC), axis=1) + v[ROWS:FULL]
            v = (v * (1.0 / CELLS)).astype(bf16)
            if half == 0:
                spill[:, at] = v
            else:
                own[:, at] = v

    for i in range(FOLD + 2):
        cin[i, 0] = jnp.zeros((SLOTS, inner), bf16)
        cin[i, SIDE + 1] = jnp.zeros((SLOTS, inner), bf16)
    if comm:

        @pl.when(ex.z >= LAYERS // 2)
        def _():
            ex.post(False)

    for k in range(chunks):
        ready(k)
        gather(0, k)
        gather(1, k)
        if k == chunks - 1:
            for c in fetched[2:]:
                c.wait()
        reduce(0, k)
        reduce(1, k)
        if comm and k == 0:

            @pl.when((ex.z > 0) & (ex.z < LAYERS // 2))
            def _():
                ex.post(False)

    fold(0)
    for a in range(3):
        ready(chunks + a)
        taps(0, a)
    if comm:

        @pl.when(ex.hub)
        def _():
            ex.post(True)

    ready(chunks + 3)
    expand(0)
    if comm:

        @pl.when(ex.rank < ex.total - 1)
        def _():
            moved().start()

    fold(1)
    for a in range(3):
        taps(1, a)
        if comm and a == 1:

            @pl.when(ex.hub)
            def _():
                ex.collect()

    expand(1)

    if comm:

        @pl.when(ex.hub)
        def _():
            ex.settle()

        @pl.when(jnp.logical_not(ex.hub))
        def _():
            ex.result()

        backlog = ex.offset() - ex.rank * HALF

        @pl.when(ex.rank > 0)
        def _():
            moved().wait_recv()

        @pl.when(ex.rank == 0)
        def _():
            arrived[...] = own[...]

        prior = arrived[...]
    else:
        backlog = jnp.full((1, 1), 3, jnp.int32)
        prior = spill[...]
    both = jnp.concatenate([prior.astype(f32), own[...].astype(f32)], axis=0).astype(bf16)
    row = lax.broadcasted_iota(jnp.int32, (HALF, SLOTS), 0)
    col = lax.broadcasted_iota(jnp.int32, (HALF, SLOTS), 1)
    pick = jnp.where(col - row == HALF - backlog, 1.0, 0.0).astype(bf16)
    out[...] = dot(pick, both).astype(bf16)
    if comm:

        @pl.when(ex.rank < ex.total - 1)
        def _():
            moved().wait_send()


        @pl.when(ex.hub)
        def _():
            ex.close(True)

        @pl.when(jnp.logical_not(ex.hub))
        def _():
            ex.close(False)


def on_device(comm, groups, tiles, tissue_index, tissue_count, wr, sr, br, ws, ss, bs, we, se, be):
    cand, cells, channels = tiles.shape
    inner = wr.shape[1]
    vmem = pl.BlockSpec(memory_space=pltpu.VMEM)
    hbm = pl.BlockSpec(memory_space=pl.ANY)
    dma = pltpu.SemaphoreType.DMA
    return pl.pallas_call(
        functools.partial(kernel, comm, groups),
        out_shape=pltpu.VMEM((HALF, channels), bf16),
        in_specs=[hbm] * 12,
        out_specs=vmem,
        scratch_shapes=[
            [
                pltpu.SMEM((1, cand), jnp.int32),
                pltpu.SMEM((1,), jnp.int32),
            ]
            + [pltpu.VMEM((inner,), f32)] * 4
            + [pltpu.VMEM((channels,), f32)] * 2,
            [pltpu.VMEM((cand, cells, KC), bf16)] * (channels // KC),
            pltpu.VMEM((channels, inner), bf16),
            pltpu.VMEM((3, 3, inner, inner), bf16),
            pltpu.VMEM((inner, channels), bf16),
            pltpu.VMEM((2, FULL, channels), bf16),
            pltpu.VMEM((HALF, channels), f32),
            pltpu.VMEM((FOLD * SIDE * SLOTS, inner), f32),
            pltpu.VMEM((2, inner // LANES, FULL, LANES), f32),
            pltpu.VMEM((FOLD + 2, SIDE + 2, SLOTS, inner), bf16),
            pltpu.VMEM((FULL, inner), bf16),
            pltpu.VMEM((HALF, channels), bf16),
            pltpu.VMEM((HALF, channels), bf16),
            pltpu.VMEM((HALF, channels), bf16),
            pltpu.VMEM((1, 128), jnp.int32),
            pltpu.VMEM((groups * LAYERS, 1, 128), jnp.int32),
            pltpu.VMEM((1, 128), jnp.int32),
            pltpu.VMEM((ROW, 1, 128), jnp.int32),
            pltpu.VMEM((2, 1, 128), jnp.int32),
            dma((8,)),
            dma((channels // KC,)),
            dma((channels // KC,)),
            dma((3,)),
            dma,
            [
                dma((groups,)),
                dma,
                dma((ROW - 1,)),
                dma,
                dma((LAYERS - 1,)),
                dma,
            ],
            dma,
            dma,
        ],
        compiler_params=pltpu.CompilerParams(
            collective_id=0 if comm else None,
            has_side_effects=True,
            vmem_limit_bytes=56 * 1024 * 1024,
        ),
        name="bottleneck",
    )(tissue_index, tissue_count, tiles, wr, sr, br, ws, ss, bs, we, se, be)


def solution(mesh):
    axes = ("grp", "ext")
    split = P(axes)
    return jax.shard_map(
        functools.partial(on_device, True, mesh.shape["grp"]),
        mesh=mesh,
        in_specs=(split, split, split) + (P(),) * 9,
        out_specs=split,
        check_vma=False,
    )
```

```python
import functools

import jax
import jax.numpy as jnp
from jax import lax
from jax.experimental import pallas as pl
from jax.experimental.pallas import tpu as pltpu
from jax.sharding import PartitionSpec as P

MESH = pl.DeviceIdType.MESH
SIDE = 7
CELLS = SIDE * SIDE
HALF = 8
SLOTS = 2 * HALF
BODY = 48
ROWS = HALF * BODY
FULL = ROWS + HALF
FOLD = 4
KC = 512
NC = 256
LAYERS = 8
AHEAD = 4
ROW = 8
LANES = 128
bf16 = jnp.bfloat16
f32 = jnp.float32


def dot(a, b):
    return jnp.dot(a, b, preferred_element_type=jnp.float32)


class Exchange:
    def __init__(self, groups, cnt, box, table, tables, answer, sems):
        self.cnt, self.box, self.table, self.tables, self.answer = cnt, box, table, tables, answer
        self.post_send, self.post_recv, self.row_send, self.row_recv, self.out_send, self.out_recv = sems
        self.groups = groups
        g = self.g = lax.axis_index("grp")
        e = lax.axis_index("ext")
        ext = lax.axis_size("ext")
        self.z = e // ROW
        self.q = lax.rem(e, ROW)
        self.rank = g * ext + e
        total = self.total = groups * ext
        self.hub = self.z == 0
        after = lax.rem(self.rank + 1, total)
        before = lax.rem(self.rank + total - 1, total)
        self.ahead = (after // ext, lax.rem(after, ext))
        self.behind = (before // ext, lax.rem(before, ext))
        self.mates = [lax.rem(self.q + k, ROW) for k in range(1, ROW)]

    def greet(self):
        barrier = pltpu.get_barrier_semaphore()

        def tell(who):
            pl.semaphore_signal(barrier, inc=1, device_id=who, device_id_type=MESH)

        @pl.when(self.hub)
        def _():
            for y in reversed(range(self.groups)):

                @pl.when(y < self.g)
                def _():
                    tell((y, self.q))

                @pl.when(y <= self.g)
                def _():
                    for z in reversed(range(1, LAYERS)):
                        tell((y, z * ROW + self.q))

            for o in self.mates:
                tell((self.g, o))

        @pl.when(jnp.logical_not(self.hub))
        def _():
            tell((self.g, self.q))

        tell(self.behind)

    def to_hub(self, y):
        return pltpu.make_async_remote_copy(
            src_ref=self.cnt,
            dst_ref=self.box.at[self.g * LAYERS + self.z],
            send_sem=self.post_send.at[y],
            recv_sem=self.post_recv,
            device_id=(y, self.q),
            device_id_type=MESH,
        )

    def each_hub(self, hub, act):
        for y in range(self.groups):

            @pl.when(y > self.g if hub else y >= self.g)
            def _():
                act(self.to_hub(y))

    def post(self, hub):
        own = ROW - 1 + LAYERS - 1 if hub else 1
        pl.semaphore_wait(pltpu.get_barrier_semaphore(), self.groups - 1 - self.g + own + 1)
        self.each_hub(hub, lambda c: c.start())

    def sent(self, hub):
        self.each_hub(hub, lambda c: c.wait_send())

    def all_of(self, box, count, sem):
        rows = box.at[pl.ds(0, count - 1)]
        pltpu.make_async_copy(rows, rows, sem).wait()

    def collect(self):
        for y in range(self.groups):

            @pl.when(y == self.g)
            def _():
                self.all_of(self.box, (y + 1) * LAYERS, self.post_recv)

        self.box[self.g * LAYERS] = self.cnt[...]
        lane = lax.broadcasted_iota(jnp.int32, (1, 128), 1)
        lower = jnp.zeros((1, 128), jnp.int32)
        for y in range(self.groups - 1):
            plane = self.box[y * LAYERS]
            for z in range(1, LAYERS):
                plane = plane + self.box[y * LAYERS + z]
            lower = lower + jnp.where(y < self.g, plane, 0)
        table = jnp.where(lane == LAYERS, lower, 0)
        for z in range(LAYERS):
            table = jnp.where(lane == z, self.box[self.g * LAYERS + z], table)
        self.table[...] = table
        for k, o in enumerate(self.mates):
            self.to_mate(k, o).start()

    def to_mate(self, k, o):
        return pltpu.make_async_remote_copy(
            src_ref=self.table,
            dst_ref=self.tables.at[self.q],
            send_sem=self.row_send.at[k],
            recv_sem=self.row_recv,
            device_id=(self.g, o),
            device_id_type=MESH,
        )

    def to_plane(self, z):
        return pltpu.make_async_remote_copy(
            src_ref=self.answer,
            dst_ref=self.answer,
            send_sem=self.out_send.at[z - 1],
            recv_sem=self.out_recv,
            device_id=(self.g, z * ROW + self.q),
            device_id_type=MESH,
        )

    def settle(self):
        self.all_of(self.tables, ROW, self.row_recv)
        mine = self.table[...]
        whole = mine
        left = jnp.zeros((1, 128), jnp.int32)
        for o in range(ROW):
            value = jnp.where(o == self.q, 0, self.tables[o])
            whole = whole + value
            left = left + jnp.where(o < self.q, value, 0)
        self.answer[0] = whole
        self.answer[1] = left
        for z in range(1, LAYERS):
            self.to_plane(z).start()

    def result(self):
        self.to_plane(1).wait_recv()

    def offset(self):
        lane = lax.broadcasted_iota(jnp.int32, (1, 128), 1)
        take = jnp.where((lane < self.z) | (lane == LAYERS), self.answer[0], 0)
        take = take + jnp.where(lane == self.z, self.answer[1], 0)
        return jnp.sum(take, axis=1, keepdims=True)

    def close(self, hub):
        self.sent(hub)
        if hub:
            for k, o in enumerate(self.mates):
                self.to_mate(k, o).wait_send()
            for z in range(1, LAYERS):
                self.to_plane(z).wait_send()


def kernel(
    comm,
    groups,
    ti_hbm,
    tc_hbm,
    x_hbm,
    wr_hbm,
    sr_hbm,
    br_hbm,
    ws_hbm,
    ss_hbm,
    bs_hbm,
    we_hbm,
    se_hbm,
    be_hbm,
    out,
    small,
    x,
    wr,
    ws,
    we,
    xs,
    last,
    acc,
    flat,
    cin,
    spat,
    own,
    spill,
    arrived,
    cnt,
    box,
    table,
    tables,
    answer,
    small_sem,
    x_sem,
    wr_sem,
    ws_sem,
    we_sem,
    sems,
    spill_send,
    spill_recv,
):
    channels = x_hbm.shape[2]
    inner = wr_hbm.shape[1]
    chunks = channels // KC

    if comm:
        ex = Exchange(groups, cnt, box, table, tables, answer, sems)

    ti, tc, sr, br, ss, bs, se, be = small
    fetched = [
        pltpu.make_async_copy(a, b, small_sem.at[n])
        for n, (a, b) in enumerate(
            zip((ti_hbm, tc_hbm, sr_hbm, br_hbm, ss_hbm, bs_hbm, se_hbm, be_hbm), small)
        )
    ]
    units = []
    for k in range(chunks):
        at = pl.ds(k * KC, KC)
        units.append(
            [
                pltpu.make_async_copy(x_hbm.at[:, :, at], x[k], x_sem.at[k]),
                pltpu.make_async_copy(wr_hbm.at[at], wr.at[at], wr_sem.at[k]),
            ]
        )
    for a in range(3):
        units.append([pltpu.make_async_copy(ws_hbm.at[a], ws.at[a], ws_sem.at[a])])
    units.append([pltpu.make_async_copy(we_hbm, we, we_sem)])

    def begin(n):
        if n < len(units):
            for c in units[n]:
                c.start()

    def ready(n):
        for c in units[n]:
            c.wait()
        begin(n + AHEAD)

    for c in fetched[:2]:
        c.start()
    for n in range(AHEAD):
        begin(n)
    for c in fetched[2:]:
        c.start()
    if comm:
        ex.greet()
    for c in fetched[:2]:
        c.wait()

    count = tc[0]
    if comm:
        cnt[...] = jnp.full((1, 128), count, jnp.int32)

    def moved():
        return pltpu.make_async_remote_copy(
            src_ref=spill,
            dst_ref=arrived,
            send_sem=spill_send,
            recv_sem=spill_recv,
            device_id=ex.ahead,
            device_id_type=MESH,
        )

    def gather(half, k):
        if half == 0:
            slots = [jnp.clip(count - HALF + j, 0, SLOTS - 1) for j in range(HALF)]
        else:
            slots = list(range(HALF))
        at = pl.ds(k * KC, KC)
        for s, slot in enumerate(slots):
            tile = ti[0, slot]
            xs[half, s * BODY : (s + 1) * BODY, at] = x[k][tile, 0:BODY, :]
            last[s : s + 1, at] = x[k][tile, BODY:CELLS, :].astype(f32)
        xs[half, ROWS:FULL, at] = last[:, at].astype(bf16)

    def reduce(half, k):
        at = pl.ds(k * KC, KC)
        part = dot(xs[half, :, at], wr[at, :])
        if k > 0:
            part = part + flat_rows(half)
        if k == chunks - 1:
            part = jnp.maximum(part * sr[...][None, :] + br[...][None, :], 0.0)
        for j in range(inner // LANES):
            flat[half, j] = part[:, j * LANES : (j + 1) * LANES]

    def flat_rows(half):
        return jnp.concatenate([flat[half, j] for j in range(inner // LANES)], axis=1)

    def fold(half):
        none = jnp.zeros((HALF, inner), f32)

        def cell(i, k):
            c = i * SIDE + k
            if i >= SIDE:
                return none
            at = pl.ds(ROWS, HALF) if c == BODY else pl.ds(c, HALF, stride=BODY)
            return jnp.concatenate([flat[half, j, at, :] for j in range(inner // LANES)], axis=1)

        for k in range(SIDE):
            for i in range(FOLD):
                low, high = cell(i, k), cell(i + FOLD, k)
                cin[i + 1, k + 1] = jnp.concatenate([low, high], axis=0).astype(bf16)
                if i == FOLD - 1:
                    cin[0, k + 1] = jnp.concatenate([none, low], axis=0).astype(bf16)
                if i == 0:
                    cin[FOLD + 1, k + 1] = jnp.concatenate([high, none], axis=0).astype(bf16)

    def taps(half, a):
        lhs = jnp.concatenate(
            [
                cin[a : a + FOLD, b : b + SIDE].reshape(FOLD * SIDE * SLOTS, inner)
                for b in range(3)
            ],
            axis=1,
        )
        part = dot(lhs, ws[a].reshape(3 * inner, inner))
        if a > 0:
            part = part + acc[...]
        if a < 2:
            acc[...] = part
            return
        part = jnp.maximum(part * ss[...][None, :] + bs[...][None, :], 0.0)
        for i in range(FOLD):
            for k in range(SIDE):
                for up in range(2):
                    v = (i * SIDE + k) * SLOTS + up * HALF
                    c = (i + up * FOLD) * SIDE + k
                    if c > BODY:
                        continue
                    at = pl.ds(ROWS, HALF) if c == BODY else pl.ds(c, HALF, stride=BODY)
                    for j in range(inner // LANES):
                        flat[half, j, at, :] = part[v : v + HALF, j * LANES : (j + 1) * LANES]
        for j in range(inner // LANES):
            spat[:, j * LANES : (j + 1) * LANES] = flat[half, j].astype(bf16)

    def expand(half):
        for n in range(channels // NC):
            at = pl.ds(n * NC, NC)
            v = dot(spat[...], we[:, at]) * se[at][None, :] + be[at][None, :]
            v = jnp.maximum(v + xs[half, :, at].astype(f32), 0.0)
            v = jnp.sum(v[:ROWS].reshape(HALF, BODY, NC), axis=1) + v[ROWS:FULL]
            v = (v * (1.0 / CELLS)).astype(bf16)
            if half == 0:
                spill[:, at] = v
            else:
                own[:, at] = v

    for i in range(FOLD + 2):
        cin[i, 0] = jnp.zeros((SLOTS, inner), bf16)
        cin[i, SIDE + 1] = jnp.zeros((SLOTS, inner), bf16)
    if comm:

        @pl.when(ex.z >= LAYERS // 2)
        def _():
            ex.post(False)

    for k in range(chunks):
        ready(k)
        gather(0, k)
        gather(1, k)
        if k == chunks - 1:
            for c in fetched[2:]:
                c.wait()
        reduce(0, k)
        reduce(1, k)
        if comm and k == 0:

            @pl.when((ex.z > 0) & (ex.z < LAYERS // 2))
            def _():
                ex.post(False)

    fold(0)
    for a in range(3):
        ready(chunks + a)
        taps(0, a)
    if comm:

        @pl.when(ex.hub)
        def _():
            ex.post(True)

    ready(chunks + 3)
    expand(0)
    if comm:

        @pl.when(ex.rank < ex.total - 1)
        def _():
            moved().start()

    fold(1)
    for a in range(3):
        taps(1, a)
        if comm and a == 1:

            @pl.when(ex.hub)
            def _():
                ex.collect()

    expand(1)

    if comm:

        @pl.when(ex.hub)
        def _():
            ex.settle()

        @pl.when(jnp.logical_not(ex.hub))
        def _():
            ex.result()

        backlog = ex.offset() - ex.rank * HALF
    else:
        backlog = jnp.full((1, 1), 3, jnp.int32)
    row = lax.broadcasted_iota(jnp.int32, (HALF, HALF), 0)
    col = lax.broadcasted_iota(jnp.int32, (HALF, HALF), 1)
    stay = dot(jnp.where(col - row == -backlog, 1.0, 0.0), own[...].astype(f32))
    come = jnp.where(col - row == HALF - backlog, 1.0, 0.0)
    if comm:

        @pl.when(ex.rank > 0)
        def _():
            moved().wait_recv()

        @pl.when(ex.rank == 0)
        def _():
            arrived[...] = own[...]

        prior = arrived[...]
    else:
        prior = spill[...]
    out[...] = (stay + dot(come, prior.astype(f32))).astype(bf16)
    if comm:

        @pl.when(ex.rank < ex.total - 1)
        def _():
            moved().wait_send()


        @pl.when(ex.hub)
        def _():
            ex.close(True)

        @pl.when(jnp.logical_not(ex.hub))
        def _():
            ex.close(False)


def on_device(comm, groups, tiles, tissue_index, tissue_count, wr, sr, br, ws, ss, bs, we, se, be):
    cand, cells, channels = tiles.shape
    inner = wr.shape[1]
    vmem = pl.BlockSpec(memory_space=pltpu.VMEM)
    hbm = pl.BlockSpec(memory_space=pl.ANY)
    dma = pltpu.SemaphoreType.DMA
    return pl.pallas_call(
        functools.partial(kernel, comm, groups),
        out_shape=pltpu.VMEM((HALF, channels), bf16),
        in_specs=[hbm] * 12,
        out_specs=vmem,
        scratch_shapes=[
            [
                pltpu.SMEM((1, cand), jnp.int32),
                pltpu.SMEM((1,), jnp.int32),
            ]
            + [pltpu.VMEM((inner,), f32)] * 4
            + [pltpu.VMEM((channels,), f32)] * 2,
            [pltpu.VMEM((cand, cells, KC), bf16)] * (channels // KC),
            pltpu.VMEM((channels, inner), bf16),
            pltpu.VMEM((3, 3, inner, inner), bf16),
            pltpu.VMEM((inner, channels), bf16),
            pltpu.VMEM((2, FULL, channels), bf16),
            pltpu.VMEM((HALF, channels), f32),
            pltpu.VMEM((FOLD * SIDE * SLOTS, inner), f32),
            pltpu.VMEM((2, inner // LANES, FULL, LANES), f32),
            pltpu.VMEM((FOLD + 2, SIDE + 2, SLOTS, inner), bf16),
            pltpu.VMEM((FULL, inner), bf16),
            pltpu.VMEM((HALF, channels), bf16),
            pltpu.VMEM((HALF, channels), bf16),
            pltpu.VMEM((HALF, channels), bf16),
            pltpu.VMEM((1, 128), jnp.int32),
            pltpu.VMEM((groups * LAYERS, 1, 128), jnp.int32),
            pltpu.VMEM((1, 128), jnp.int32),
            pltpu.VMEM((ROW, 1, 128), jnp.int32),
            pltpu.VMEM((2, 1, 128), jnp.int32),
            dma((8,)),
            dma((channels // KC,)),
            dma((channels // KC,)),
            dma((3,)),
            dma,
            [
                dma((groups,)),
                dma,
                dma((ROW - 1,)),
                dma,
                dma((LAYERS - 1,)),
                dma,
            ],
            dma,
            dma,
        ],
        compiler_params=pltpu.CompilerParams(
            collective_id=0 if comm else None,
            has_side_effects=True,
            vmem_limit_bytes=56 * 1024 * 1024,
        ),
        name="bottleneck",
    )(tissue_index, tissue_count, tiles, wr, sr, br, ws, ss, bs, we, se, be)


def solution(mesh):
    axes = ("grp", "ext")
    split = P(axes)
    return jax.shard_map(
        functools.partial(on_device, True, mesh.shape["grp"]),
        mesh=mesh,
        in_specs=(split, split, split) + (P(),) * 9,
        out_specs=split,
        check_vma=False,
    )
```

```python
import functools

import jax
import jax.numpy as jnp
from jax import lax
from jax.experimental import pallas as pl
from jax.experimental.pallas import tpu as pltpu
from jax.sharding import PartitionSpec as P

MESH = pl.DeviceIdType.MESH
SIDE = 7
CELLS = SIDE * SIDE
HALF = 8
SLOTS = 2 * HALF
BODY = 48
ROWS = HALF * BODY
FULL = ROWS + HALF
FOLD = 4
KC = 512
NC = 256
LAYERS = 8
AHEAD = 4
ROW = 8
LANES = 128
bf16 = jnp.bfloat16
f32 = jnp.float32


def dot(a, b):
    return jnp.dot(a, b, preferred_element_type=jnp.float32)


class Exchange:
    def __init__(self, groups, cnt, box, table, tables, answer, sems):
        self.cnt, self.box, self.table, self.tables, self.answer = cnt, box, table, tables, answer
        self.post_send, self.post_recv, self.row_send, self.row_recv, self.out_send, self.out_recv = sems
        self.groups = groups
        g = self.g = lax.axis_index("grp")
        e = lax.axis_index("ext")
        ext = lax.axis_size("ext")
        self.z = e // ROW
        self.q = lax.rem(e, ROW)
        self.rank = g * ext + e
        total = self.total = groups * ext
        self.hub = self.z == 0
        after = lax.rem(self.rank + 1, total)
        before = lax.rem(self.rank + total - 1, total)
        self.ahead = (after // ext, lax.rem(after, ext))
        self.behind = (before // ext, lax.rem(before, ext))
        self.mates = [lax.rem(self.q + k, ROW) for k in range(1, ROW)]

    def greet(self):
        barrier = pltpu.get_barrier_semaphore()

        def tell(who):
            pl.semaphore_signal(barrier, inc=1, device_id=who, device_id_type=MESH)

        @pl.when(self.hub)
        def _():
            for y in reversed(range(self.groups)):

                @pl.when(y < self.g)
                def _():
                    tell((y, self.q))

                @pl.when(y <= self.g)
                def _():
                    for z in reversed(range(1, LAYERS)):
                        tell((y, z * ROW + self.q))

            for o in self.mates:
                tell((self.g, o))

        @pl.when(jnp.logical_not(self.hub))
        def _():
            tell((self.g, self.q))

        tell(self.behind)

    def to_hub(self, y):
        return pltpu.make_async_remote_copy(
            src_ref=self.cnt,
            dst_ref=self.box.at[self.g * LAYERS + self.z],
            send_sem=self.post_send.at[y],
            recv_sem=self.post_recv,
            device_id=(y, self.q),
            device_id_type=MESH,
        )

    def each_hub(self, hub, act):
        for y in range(self.groups):

            @pl.when(y > self.g if hub else y >= self.g)
            def _():
                act(self.to_hub(y))

    def post(self, hub):
        own = ROW - 1 + LAYERS - 1 if hub else 1
        pl.semaphore_wait(pltpu.get_barrier_semaphore(), self.groups - 1 - self.g + own + 1)
        self.each_hub(hub, lambda c: c.start())

    def sent(self, hub):
        self.each_hub(hub, lambda c: c.wait_send())

    def all_of(self, box, count, sem):
        rows = box.at[pl.ds(0, count - 1)]
        pltpu.make_async_copy(rows, rows, sem).wait()

    def collect(self):
        for y in range(self.groups):

            @pl.when(y == self.g)
            def _():
                self.all_of(self.box, (y + 1) * LAYERS, self.post_recv)

        self.box[self.g * LAYERS] = self.cnt[...]
        lane = lax.broadcasted_iota(jnp.int32, (1, 128), 1)
        lower = jnp.zeros((1, 128), jnp.int32)
        for y in range(self.groups - 1):
            plane = self.box[y * LAYERS]
            for z in range(1, LAYERS):
                plane = plane + self.box[y * LAYERS + z]
            lower = lower + jnp.where(y < self.g, plane, 0)
        table = jnp.where(lane == LAYERS, lower, 0)
        for z in range(LAYERS):
            table = jnp.where(lane == z, self.box[self.g * LAYERS + z], table)
        self.table[...] = table
        for k, o in enumerate(self.mates):
            self.to_mate(k, o).start()

    def to_mate(self, k, o):
        return pltpu.make_async_remote_copy(
            src_ref=self.table,
            dst_ref=self.tables.at[self.q],
            send_sem=self.row_send.at[k],
            recv_sem=self.row_recv,
            device_id=(self.g, o),
            device_id_type=MESH,
        )

    def to_plane(self, z):
        return pltpu.make_async_remote_copy(
            src_ref=self.answer,
            dst_ref=self.answer,
            send_sem=self.out_send.at[z - 1],
            recv_sem=self.out_recv,
            device_id=(self.g, z * ROW + self.q),
            device_id_type=MESH,
        )

    def settle(self):
        self.all_of(self.tables, ROW, self.row_recv)
        mine = self.table[...]
        whole = mine
        left = jnp.zeros((1, 128), jnp.int32)
        for o in range(ROW):
            value = jnp.where(o == self.q, 0, self.tables[o])
            whole = whole + value
            left = left + jnp.where(o < self.q, value, 0)
        self.answer[0] = whole
        self.answer[1] = left
        for z in range(1, LAYERS):
            self.to_plane(z).start()

    def result(self):
        self.to_plane(1).wait_recv()

    def offset(self):
        lane = lax.broadcasted_iota(jnp.int32, (1, 128), 1)
        take = jnp.where((lane < self.z) | (lane == LAYERS), self.answer[0], 0)
        take = take + jnp.where(lane == self.z, self.answer[1], 0)
        return jnp.sum(take, axis=1, keepdims=True)

    def close(self, hub):
        self.sent(hub)
        if hub:
            for k, o in enumerate(self.mates):
                self.to_mate(k, o).wait_send()
            for z in range(1, LAYERS):
                self.to_plane(z).wait_send()


def kernel(
    comm,
    groups,
    ti_hbm,
    tc_hbm,
    x_hbm,
    wr_hbm,
    sr_hbm,
    br_hbm,
    ws_hbm,
    ss_hbm,
    bs_hbm,
    we_hbm,
    se_hbm,
    be_hbm,
    out,
    small,
    x,
    wr,
    ws,
    we,
    xs,
    last,
    acc,
    flat,
    cin,
    spat,
    own,
    spill,
    arrived,
    cnt,
    box,
    table,
    tables,
    answer,
    small_sem,
    x_sem,
    wr_sem,
    ws_sem,
    we_sem,
    sems,
    spill_send,
    spill_recv,
):
    channels = x_hbm.shape[2]
    inner = wr_hbm.shape[1]
    chunks = channels // KC

    if comm:
        ex = Exchange(groups, cnt, box, table, tables, answer, sems)

    ti, tc, sr, br, ss, bs, se, be = small
    fetched = [
        pltpu.make_async_copy(a, b, small_sem.at[n])
        for n, (a, b) in enumerate(
            zip((ti_hbm, tc_hbm, sr_hbm, br_hbm, ss_hbm, bs_hbm, se_hbm, be_hbm), small)
        )
    ]
    units = []
    for k in range(chunks):
        at = pl.ds(k * KC, KC)
        units.append(
            [
                pltpu.make_async_copy(x_hbm.at[:, :, at], x[k], x_sem.at[k]),
                pltpu.make_async_copy(wr_hbm.at[at], wr.at[at], wr_sem.at[k]),
            ]
        )
    for a in range(3):
        units.append([pltpu.make_async_copy(ws_hbm.at[a], ws.at[a], ws_sem.at[a])])
    units.append([pltpu.make_async_copy(we_hbm, we, we_sem)])

    def begin(n):
        if n < len(units):
            for c in units[n]:
                c.start()

    def ready(n):
        for c in units[n]:
            c.wait()
        begin(n + AHEAD)

    for c in fetched[:2]:
        c.start()
    for n in range(AHEAD):
        begin(n)
    for c in fetched[2:]:
        c.start()
    if comm:
        ex.greet()
    for c in fetched[:2]:
        c.wait()

    count = tc[0]
    if comm:
        cnt[...] = jnp.full((1, 128), count, jnp.int32)

    def moved(h):
        return pltpu.make_async_remote_copy(
            src_ref=spill[h],
            dst_ref=arrived[h],
            send_sem=spill_send.at[h],
            recv_sem=spill_recv.at[h],
            device_id=ex.ahead,
            device_id_type=MESH,
        )

    def gather(half, k):
        if half == 0:
            slots = [jnp.clip(count - HALF + j, 0, SLOTS - 1) for j in range(HALF)]
        else:
            slots = list(range(HALF))
        at = pl.ds(k * KC, KC)
        for s, slot in enumerate(slots):
            tile = ti[0, slot]
            xs[half, s * BODY : (s + 1) * BODY, at] = x[k][tile, 0:BODY, :]
            last[s : s + 1, at] = x[k][tile, BODY:CELLS, :].astype(f32)
        xs[half, ROWS:FULL, at] = last[:, at].astype(bf16)

    def reduce(half, k):
        at = pl.ds(k * KC, KC)
        part = dot(xs[half, :, at], wr[at, :])
        if k > 0:
            part = part + flat_rows(half)
        if k == chunks - 1:
            part = jnp.maximum(part * sr[...][None, :] + br[...][None, :], 0.0)
        for j in range(inner // LANES):
            flat[half, j] = part[:, j * LANES : (j + 1) * LANES]

    def flat_rows(half):
        return jnp.concatenate([flat[half, j] for j in range(inner // LANES)], axis=1)

    def fold(half):
        none = jnp.zeros((HALF, inner), f32)

        def cell(i, k):
            c = i * SIDE + k
            if i >= SIDE:
                return none
            at = pl.ds(ROWS, HALF) if c == BODY else pl.ds(c, HALF, stride=BODY)
            return jnp.concatenate([flat[half, j, at, :] for j in range(inner // LANES)], axis=1)

        for k in range(SIDE):
            for i in range(FOLD):
                low, high = cell(i, k), cell(i + FOLD, k)
                cin[i + 1, k + 1] = jnp.concatenate([low, high], axis=0).astype(bf16)
                if i == FOLD - 1:
                    cin[0, k + 1] = jnp.concatenate([none, low], axis=0).astype(bf16)
                if i == 0:
                    cin[FOLD + 1, k + 1] = jnp.concatenate([high, none], axis=0).astype(bf16)

    def taps(half, a):
        lhs = jnp.concatenate(
            [
                cin[a : a + FOLD, b : b + SIDE].reshape(FOLD * SIDE * SLOTS, inner)
                for b in range(3)
            ],
            axis=1,
        )
        part = dot(lhs, ws[a].reshape(3 * inner, inner))
        if a > 0:
            part = part + acc[...]
        if a < 2:
            acc[...] = part
            return
        part = jnp.maximum(part * ss[...][None, :] + bs[...][None, :], 0.0)
        for i in range(FOLD):
            for k in range(SIDE):
                for up in range(2):
                    v = (i * SIDE + k) * SLOTS + up * HALF
                    c = (i + up * FOLD) * SIDE + k
                    if c > BODY:
                        continue
                    at = pl.ds(ROWS, HALF) if c == BODY else pl.ds(c, HALF, stride=BODY)
                    for j in range(inner // LANES):
                        flat[half, j, at, :] = part[v : v + HALF, j * LANES : (j + 1) * LANES]
        for j in range(inner // LANES):
            spat[:, j * LANES : (j + 1) * LANES] = flat[half, j].astype(bf16)

    def send_spill(h):
        @pl.when(ex.rank < ex.total - 1)
        def _():
            moved(h).start()

    def expand(half):
        for n in range(channels // NC):
            at = pl.ds(n * NC, NC)
            v = dot(spat[...], we[:, at]) * se[at][None, :] + be[at][None, :]
            v = jnp.maximum(v + xs[half, :, at].astype(f32), 0.0)
            v = jnp.sum(v[:ROWS].reshape(HALF, BODY, NC), axis=1) + v[ROWS:FULL]
            v = (v * (1.0 / CELLS)).astype(bf16)
            if half == 0:
                per = channels // NC // 2
                spill[n // per][:, n % per * NC : (n % per + 1) * NC] = v
                if comm and n % per == per - 1:
                    send_spill(n // per)
            else:
                own[:, at] = v

    for i in range(FOLD + 2):
        cin[i, 0] = jnp.zeros((SLOTS, inner), bf16)
        cin[i, SIDE + 1] = jnp.zeros((SLOTS, inner), bf16)
    if comm:

        @pl.when(ex.z >= LAYERS // 2)
        def _():
            ex.post(False)

    for k in range(chunks):
        ready(k)
        gather(0, k)
        gather(1, k)
        if k == chunks - 1:
            for c in fetched[2:]:
                c.wait()
        reduce(0, k)
        reduce(1, k)
        if comm and k == 0:

            @pl.when((ex.z > 0) & (ex.z < LAYERS // 2))
            def _():
                ex.post(False)

    fold(0)
    for a in range(3):
        ready(chunks + a)
        taps(0, a)
    if comm:

        @pl.when(ex.hub)
        def _():
            ex.post(True)

    ready(chunks + 3)
    expand(0)
    fold(1)
    for a in range(3):
        taps(1, a)
        if comm and a == 1:

            @pl.when(ex.hub)
            def _():
                ex.collect()

    expand(1)

    if comm:

        @pl.when(ex.hub)
        def _():
            ex.settle()

        @pl.when(jnp.logical_not(ex.hub))
        def _():
            ex.result()

        backlog = ex.offset() - ex.rank * HALF

        @pl.when(ex.rank > 0)
        def _():
            for h in range(2):
                moved(h).wait_recv()

        @pl.when(ex.rank == 0)
        def _():
            for h in range(2):
                arrived[h][...] = jnp.zeros_like(arrived[h])

        prior = jnp.concatenate([arrived[h][...] for h in range(2)], axis=1)
    else:
        backlog = jnp.full((1, 1), 3, jnp.int32)
        prior = jnp.concatenate([spill[h][...] for h in range(2)], axis=1)
    both = jnp.concatenate([prior.astype(f32), own[...].astype(f32)], axis=0).astype(bf16)
    row = lax.broadcasted_iota(jnp.int32, (HALF, SLOTS), 0)
    col = lax.broadcasted_iota(jnp.int32, (HALF, SLOTS), 1)
    pick = jnp.where(col - row == HALF - backlog, 1.0, 0.0).astype(bf16)
    out[...] = dot(pick, both).astype(bf16)
    if comm:

        @pl.when(ex.rank < ex.total - 1)
        def _():
            for h in range(2):
                moved(h).wait_send()


        @pl.when(ex.hub)
        def _():
            ex.close(True)

        @pl.when(jnp.logical_not(ex.hub))
        def _():
            ex.close(False)


def on_device(comm, groups, tiles, tissue_index, tissue_count, wr, sr, br, ws, ss, bs, we, se, be):
    cand, cells, channels = tiles.shape
    inner = wr.shape[1]
    vmem = pl.BlockSpec(memory_space=pltpu.VMEM)
    hbm = pl.BlockSpec(memory_space=pl.ANY)
    dma = pltpu.SemaphoreType.DMA
    return pl.pallas_call(
        functools.partial(kernel, comm, groups),
        out_shape=pltpu.VMEM((HALF, channels), bf16),
        in_specs=[hbm] * 12,
        out_specs=vmem,
        scratch_shapes=[
            [
                pltpu.SMEM((1, cand), jnp.int32),
                pltpu.SMEM((1,), jnp.int32),
            ]
            + [pltpu.VMEM((inner,), f32)] * 4
            + [pltpu.VMEM((channels,), f32)] * 2,
            [pltpu.VMEM((cand, cells, KC), bf16)] * (channels // KC),
            pltpu.VMEM((channels, inner), bf16),
            pltpu.VMEM((3, 3, inner, inner), bf16),
            pltpu.VMEM((inner, channels), bf16),
            pltpu.VMEM((2, FULL, channels), bf16),
            pltpu.VMEM((HALF, channels), f32),
            pltpu.VMEM((FOLD * SIDE * SLOTS, inner), f32),
            pltpu.VMEM((2, inner // LANES, FULL, LANES), f32),
            pltpu.VMEM((FOLD + 2, SIDE + 2, SLOTS, inner), bf16),
            pltpu.VMEM((FULL, inner), bf16),
            pltpu.VMEM((HALF, channels), bf16),
            [pltpu.VMEM((HALF, channels // 2), bf16)] * 2,
            [pltpu.VMEM((HALF, channels // 2), bf16)] * 2,
            pltpu.VMEM((1, 128), jnp.int32),
            pltpu.VMEM((groups * LAYERS, 1, 128), jnp.int32),
            pltpu.VMEM((1, 128), jnp.int32),
            pltpu.VMEM((ROW, 1, 128), jnp.int32),
            pltpu.VMEM((2, 1, 128), jnp.int32),
            dma((8,)),
            dma((channels // KC,)),
            dma((channels // KC,)),
            dma((3,)),
            dma,
            [
                dma((groups,)),
                dma,
                dma((ROW - 1,)),
                dma,
                dma((LAYERS - 1,)),
                dma,
            ],
            dma((2,)),
            dma((2,)),
        ],
        compiler_params=pltpu.CompilerParams(
            collective_id=0 if comm else None,
            has_side_effects=True,
            vmem_limit_bytes=56 * 1024 * 1024,
        ),
        name="bottleneck",
    )(tissue_index, tissue_count, tiles, wr, sr, br, ws, ss, bs, we, se, be)


def solution(mesh):
    axes = ("grp", "ext")
    split = P(axes)
    return jax.shard_map(
        functools.partial(on_device, True, mesh.shape["grp"]),
        mesh=mesh,
        in_specs=(split, split, split) + (P(),) * 9,
        out_specs=split,
        check_vma=False,
    )
```
